32 devices in a mesh: vox: 32 (over z, y, x, core).
Axes of the slice: x: 2, y: 2, z: 4, core: 2. Of those that a mesh axis runs over, the one named last changes fastest.
Arguments:
- features: float32 [32768, 128], P('vox'), may hold values from -6 to 6
- kernel_one: float32 [27, 128, 128], replicated, may hold values from -0.125 to 0.125
- gain_one: float32 [128], replicated, may hold values from 0.1 to 1.9
- bias_one: float32 [128], replicated, may hold values from -3 to 3
- kernel_two: float32 [27, 128, 128], replicated, may hold values from -0.125 to 0.125
- gain_two: float32 [128], replicated, may hold values from 0.1 to 1.9
- bias_two: float32 [128], replicated, may hold values from -3 to 3
- cotangent: float32 [32768, 128], P('vox'), may hold values from -6 to 6
- cumulative: int32 [33], replicated, may hold values from 0 to 24576, as said below
- neighbours: int32 [27, 32768], P(None, 'vox'), may hold values from -1 to 1279, as said below
Outputs:
- output: float32 [32768, 128], P('vox')
- grad_features: float32 [32768, 128], P('vox')
- grad_kernel_one: float32 [27, 128, 128], replicated
- grad_kernel_two: float32 [27, 128, 128], replicated
- grad_gain_one: float32 [128], replicated
- grad_bias_one: float32 [128], replicated
- grad_gain_two: float32 [128], replicated
- grad_bias_two: float32 [128], replicated
The draws below stay inside these ranges and needn't reach their ends.
Inputs may be any that keep to these rules, and one draw needn't show every extreme that they name: `cumulative`: each device holds between 512 and 1024 live rows; some device is full in every draw; there are 24576 live rows in all. `neighbours`: entries of padding slots are -1; a live slot's entry points into the extended rows of its own device, at most 128 rows before or after it in the spatial order; the centre offset 13 always points at the row itself.
All inputs are finite; a program needn't handle non-finite values.
Results may differ from the reference program's by a relative error of at most 0.0003.
Values sent between devices are 32-bit elements; how exact they have to be, the bound alone decides.
No kernel may reach another device: no remote copies, remote signals or barrier semaphores. Data moves between devices by JAX's collectives and lax.ppermute only.
A program may use at most 64 MiB of HBM per device.

```python
import jax
import jax.numpy as jnp
from jax import lax

C = 128
KVOL = 27
CAP = 1024
HALO = 128
ROWS = 32768
N_VOX = 32


def live_counts(key):
    first_half = jax.random.randint(jax.random.fold_in(key, 11), (N_VOX // 2,), CAP // 2, CAP + 1)
    fullest = jax.random.randint(jax.random.fold_in(key, 12), (), 0, N_VOX // 2)
    first_half = jnp.where(jnp.arange(N_VOX // 2) == fullest, CAP, first_half)
    partner = 3 * CAP // 2 - first_half
    return jnp.stack([first_half, partner], 1).reshape(N_VOX).astype(jnp.int32)


def draw_cumulative(key, part):
    counts = live_counts(key)
    return jnp.concatenate([jnp.zeros((1,), jnp.int32), jnp.cumsum(counts).astype(jnp.int32)])


def draw_neighbours(key, part):
    counts = live_counts(key)
    key = jax.random.fold_in(key, 5)
    reach = jax.random.randint(jax.random.fold_in(key, 1), (KVOL, N_VOX, CAP), -HALO, HALO + 1)
    present = jax.random.randint(jax.random.fold_in(key, 2), (KVOL, N_VOX, CAP), 0, 2) == 1
    offset = jnp.arange(KVOL)[:, None, None]
    slot = jnp.arange(CAP)[None, None, :]
    count = counts[None, :, None]
    edge = (offset == KVOL - 1) & (slot == count - 1)
    reach = jnp.where(offset == 13, 0, jnp.where(edge, HALO, reach))
    present = present | (offset == 13) | edge
    place = slot + reach
    target = jnp.where(place < count, HALO + place, HALO + CAP + place - count)
    value = jnp.where(present & (slot < count), target, -1)
    return value.reshape(KVOL, N_VOX * CAP).astype(jnp.int32)


def block_scale(rng, extent, cuts, least, high):
    loudness, own = 1.0, jax.random.fold_in(rng, 6)
    for dim, parts in cuts:
        steps = jnp.exp(jax.random.uniform(jax.random.fold_in(own, dim), (parts,), jnp.float32, least / len(cuts), high / len(cuts)))
        loudness = loudness * jnp.repeat(steps, extent[dim] // parts).reshape([-1 if axis == dim else 1 for axis in range(len(extent))])
    return loudness


def gaussian(stream_key, dims, width, most, split=(), kind=jnp.bfloat16):
    array = jax.random.normal(stream_key, dims, jnp.float32) * width
    if len(split) > 0:
        array = block_scale(stream_key, dims, split, -0.22, 0.18) * array
    return jnp.clip(array, min=-most, max=most).astype(kind)


def setup_inputs(seed: int = 0) -> dict:
    keys = jax.random.split(jax.random.key(seed), 11)
    features = gaussian(keys[0], (ROWS, C), 1.0, 6.0, ((0, 32),), jnp.float32)
    kernel_one = gaussian(keys[1], (KVOL, C, C), (14 * C) ** -0.5, 0.125, (), jnp.float32)
    gain_one = jnp.clip(1.0 + 0.18 * jax.random.normal(keys[2], (C,), jnp.float32), 0.1, 1.9)
    bias_one = gaussian(keys[3], (C,), 0.5, 3.0, (), jnp.float32)
    kernel_two = gaussian(keys[4], (KVOL, C, C), (14 * C) ** -0.5, 0.125, (), jnp.float32)
    gain_two = jnp.clip(1.0 + 0.18 * jax.random.normal(keys[5], (C,), jnp.float32), 0.1, 1.9)
    bias_two = gaussian(keys[6], (C,), 0.5, 3.0, (), jnp.float32)
    cotangent = gaussian(keys[7], (ROWS, C), 1.0, 6.0, ((0, 32),), jnp.float32)
    cumulative = draw_cumulative(jax.random.fold_in(keys[10], 71), 0)
    neighbours = draw_neighbours(jax.random.fold_in(keys[10], 71), 0)
    return {"features": features, "kernel_one": kernel_one, "gain_one": gain_one, "bias_one": bias_one, "kernel_two": kernel_two, "gain_two": gain_two, "bias_two": bias_two, "cotangent": cotangent, "cumulative": cumulative, "neighbours": neighbours}


@jax.custom_vjp
def low(v):
    return lax.optimization_barrier(v.astype(jnp.bfloat16)).astype(jnp.float32)

@jax.custom_vjp
def low_back(v):
    return v

def low_keep(v):
    return (low(v), None)

def low_pass(kept, grad):
    return (grad,)

def back_keep(v):
    return (v, None)

def back_low(kept, grad):
    return (low(grad),)
low.defvjp(low_keep, low_pass)
low_back.defvjp(back_keep, back_low)

def extend(field, counts):
    upper = jax.vmap(lambda piece, count: lax.dynamic_slice_in_dim(piece, (count - HALO).astype(jnp.int32), HALO, 0))(field, counts)
    lower = field[:, :HALO]
    zero = jnp.zeros((1, HALO, C), jnp.float32)
    before = jnp.concatenate([zero, upper[:-1]], 0)
    after = jnp.concatenate([lower[1:], zero], 0)
    extra = jnp.zeros((N_VOX, 1, C), jnp.float32)
    return jnp.concatenate([before, field, after, extra], 1)

def device_conv(padded, slots, kernel):

    def step(total, pair):
        index, matrix = pair
        taken = padded[index]
        return (total + jnp.dot(taken, matrix, precision=lax.Precision.HIGHEST, preferred_element_type=jnp.float32), None)
    total, unused = lax.scan(step, jnp.zeros((CAP, C), jnp.float32), (slots, kernel))
    return total

def convolve(field, counts, slots, kernel):
    padded = extend(field, counts)
    return lax.map(jax.checkpoint(lambda pair: device_conv(pair[0], pair[1], kernel)), (padded, slots))

def batch_norm(values, mask, total, gain, bias):
    mean = lax.optimization_barrier(jnp.sum(mask * values, (0, 1))) / total
    centred = values - mean
    spread = lax.optimization_barrier(jnp.sum(mask * centred * centred, (0, 1))) / total
    return centred * lax.rsqrt(spread + 1e-05) * gain + bias

def reference(features, kernel_one, gain_one, bias_one, kernel_two, gain_two, bias_two, cotangent, cumulative, neighbours):
    counts = cumulative[1:] - cumulative[:-1]
    total = cumulative[N_VOX].astype(jnp.float32)
    mask = (jnp.arange(CAP)[None, :] < counts[:, None]).astype(jnp.float32)[:, :, None]
    extended_rows = CAP + 2 * HALO
    slots = jnp.where(neighbours < 0, extended_rows, neighbours).reshape(KVOL, N_VOX, CAP)
    slots = jnp.transpose(slots, (1, 0, 2)).astype(jnp.int32)

    def forward(inputs, kernel_a, gain_a, bias_a, kernel_b, gain_b, bias_b):
        field = inputs.reshape(N_VOX, CAP, C)
        first = convolve(field, counts, slots, kernel_a)
        hidden = mask * jax.nn.silu(batch_norm(first, mask, total, gain_a, bias_a))
        second = convolve(hidden, counts, slots, kernel_b)
        pre = batch_norm(second, mask, total, gain_b, bias_b) + field
        return (mask * jax.nn.silu(pre)).reshape(N_VOX * CAP, C)
    output, pullback = jax.vjp(forward, features, kernel_one, gain_one, bias_one, kernel_two, gain_two, bias_two)
    grads = pullback(cotangent)
    return (output, grads[0], grads[1], grads[4], grads[2], grads[3], grads[5], grads[6])
```

```python
import functools

import jax
import jax.numpy as jnp
from jax import lax
from jax.experimental import pallas as pl
from jax.experimental.pallas import tpu as pltpu
from jax.sharding import PartitionSpec as P

HALO = 128
BLOCK = 256
SPAN = BLOCK + 2 * HALO
EPS = 1e-05
F32 = jnp.float32
BF16 = jnp.bfloat16


def split(values):
    high = values.astype(BF16)
    low = (values - high.astype(F32)).astype(BF16)
    return (high, low)


def silu_slope(values):
    sigma = jax.nn.sigmoid(values)
    return sigma * (1.0 + values * (1.0 - sigma))


def row_mask(rows, live):
    return lax.broadcasted_iota(jnp.int32, (rows, 1), 0) < live


def place(ref, before, own, after, live):
    rows = own.shape[0]
    ref[:HALO, :] = before
    ref[HALO : HALO + rows, :] = own
    ref[HALO + rows :, :] = jnp.zeros((HALO, own.shape[1]), F32)
    ref[pl.ds(HALO + live, HALO), :] = after


def one_hot(index, rows, axis):
    shape = (rows, SPAN) if axis == 1 else (rows, index.shape[1])
    return (index == lax.broadcasted_iota(jnp.int32, shape, axis)).astype(F32).astype(BF16)


def gather_conv(ext, index_ref, kernel_ref, halves, taken, turned, live):
    offsets, width = kernel_ref.shape[0], kernel_ref.shape[2]
    rows = index_ref.shape[1]
    high, low = split(ext[...])
    halves[:, :width] = high
    halves[:, width:] = low
    index = index_ref[...]
    index = jnp.where(index >= HALO + rows, index - rows + live, index)
    turned[:offsets, :] = index
    turned[offsets:, :] = jnp.full((turned.shape[0] - offsets, rows), -1, jnp.int32)
    for b in range(rows // BLOCK):
        window = halves[BLOCK * b : BLOCK * b + SPAN, :]
        columns = jnp.concatenate(
            [
                turned[:, BLOCK * b + HALO * h : BLOCK * b + HALO * (h + 1)].T
                for h in range(BLOCK // HALO)
            ],
            0,
        ) - (BLOCK * b)
        for k in range(offsets):
            hit = one_hot(columns[:, k : k + 1], BLOCK, 1)
            taken[k, BLOCK * b : BLOCK * (b + 1), :] = jnp.dot(
                hit, window, preferred_element_type=F32
            ).astype(BF16)
    total = jnp.zeros((rows, 2 * width), F32)
    for k in range(offsets):
        high, low = split(kernel_ref[k])
        wide = jnp.concatenate([high, low], 1)
        total = total + jnp.dot(
            taken[k], jnp.concatenate([wide, wide], 0), preferred_element_type=F32
        )
    return total[:, :width] + total[:, width:]


def scatter_conv(halves, target_ref, kernel_ref, field_turned, grad_kernel_ref, dfield):
    offsets, width = kernel_ref.shape[0], kernel_ref.shape[2]
    rows = dfield.shape[0]
    total = jnp.zeros((rows, 2 * width), F32)
    for k in range(offsets):
        pieces = []
        for b in range(rows // BLOCK):
            index = target_ref[k : k + 1, BLOCK * b : BLOCK * b + SPAN] - BLOCK * b
            hit = one_hot(index, BLOCK, 0)
            got = jnp.dot(
                hit, halves[BLOCK * b : BLOCK * b + SPAN, :], preferred_element_type=F32
            )
            high, low = split(got[:, :width] + got[:, width:])
            pieces.append(jnp.concatenate([high, low], 1))
        spread = jnp.concatenate(pieces, 0)
        high, low = split(kernel_ref[k])
        tall = jnp.concatenate([high, low], 0)
        total = total + lax.dot_general(
            spread,
            jnp.concatenate([tall, tall], 1),
            (((1,), (1,)), ((), ())),
            preferred_element_type=F32,
        )
        outer = jnp.dot(field_turned, spread, preferred_element_type=F32)
        outer = outer[:, :width] + outer[:, width:]
        grad_kernel_ref[k] = outer[:width] + outer[width:]
    dfield[...] = total[:, :width] + total[:, width:]


def norm_stats(gathered_ref, cumulative_ref):
    count = gathered_ref.shape[0]
    total = cumulative_ref[count].astype(F32)
    mean = jnp.sum(gathered_ref[:, 0:1, :], 0) / total

    def step(d, spread):
        live = (cumulative_ref[d + 1] - cumulative_ref[d]).astype(F32)
        own = gathered_ref[d, 0:1, :] / live - mean
        return spread + gathered_ref[d, 1:2, :] + live * own * own

    spread = lax.fori_loop(0, count, step, jnp.zeros_like(mean))
    return (mean, lax.rsqrt(spread / total + EPS))


def share(stats_ref, first, second):
    both = jnp.concatenate([first, second], 0)
    stats_ref[...] = jnp.broadcast_to(both[None], stats_ref.shape)


def conv_stats(y, mask, live, stats_ref):
    first = jnp.sum(y, 0, keepdims=True)
    centred = jnp.where(mask, y - first / live.astype(F32), 0.0)
    share(stats_ref, first, jnp.sum(centred * centred, 0, keepdims=True))


def edges(head_ref, tail_ref, ref, live):
    head_ref[...] = ref[:HALO, :]
    tail_ref[...] = ref[pl.ds(live - HALO, HALO), :]


def first_kernel(
    place_ref, x_ref, before_ref, after_ref, index_ref, kernel_ref,
    y_ref, head_ref, tail_ref, stats_ref,
    ext, halves, taken, turned,
):
    live = place_ref[1]
    place(ext, before_ref[...], x_ref[...], after_ref[...], live)
    y = gather_conv(ext, index_ref, kernel_ref, halves, taken, turned, live)
    y_ref[...] = y
    conv_stats(y, row_mask(y.shape[0], live), live, stats_ref)
    edges(head_ref, tail_ref, y_ref, live)


def second_kernel(
    place_ref, cumulative_ref, y1_ref, before_ref, after_ref, gathered_ref, gain_ref, bias_ref,
    index_ref, kernel_ref,
    y_ref, head_ref, tail_ref, stats_ref, hidden_ref,
    ext, halves, taken, turned,
):
    rank, live, count = place_ref[0], place_ref[1], gathered_ref.shape[0]
    mean, scale = norm_stats(gathered_ref, cumulative_ref)
    rows = y1_ref.shape[0]
    mask = row_mask(rows, live)

    def act(y):
        a = (y - mean) * scale * gain_ref[...] + bias_ref[...]
        return a * jax.nn.sigmoid(a)

    own = jnp.where(mask, act(y1_ref[...]), 0.0)
    hidden_ref[...] = own
    before = jnp.where(rank > 0, act(before_ref[...]), 0.0)
    after = jnp.where(rank < count - 1, act(after_ref[...]), 0.0)
    place(ext, before, own, after, live)
    y = gather_conv(ext, index_ref, kernel_ref, halves, taken, turned, live)
    y_ref[...] = y
    conv_stats(y, mask, live, stats_ref)
    edges(head_ref, tail_ref, y_ref, live)


def middle_kernel(
    place_ref, cumulative_ref, y_ref, y_before_ref, y_after_ref, gathered_ref, gain_ref, bias_ref,
    x_ref, before_ref, after_ref, cotangent_ref,
    out_ref, dz_ref, unit_ref, stats_ref,
):
    live = place_ref[1]
    mean, scale = norm_stats(gathered_ref, cumulative_ref)
    mask = row_mask(x_ref.shape[0], live)

    def part(y, x, cotangent):
        unit = (y - mean) * scale
        pre = unit * gain_ref[...] + bias_ref[...] + x
        return (unit, pre, cotangent * silu_slope(pre))

    unit, pre, dz = part(y_ref[...], x_ref[...], cotangent_ref[...])
    dz = jnp.where(mask, dz, 0.0)
    out_ref[...] = jnp.where(mask, pre * jax.nn.sigmoid(pre), 0.0)
    share(
        stats_ref, jnp.sum(dz, 0, keepdims=True), jnp.sum(dz * unit, 0, keepdims=True)
    )
    unit_b, _, dz_b = part(y_before_ref[...], before_ref[:HALO, :], before_ref[HALO : 2 * HALO, :])
    unit_a, _, dz_a = part(y_after_ref[...], after_ref[:HALO, :], after_ref[HALO : 2 * HALO, :])
    place(dz_ref, dz_b, dz, dz_a, live)
    place(unit_ref, unit_b, unit, unit_a, live)


def norm_back(dz, unit, scale, gain, gathered_ref, total):
    dbias = jnp.sum(gathered_ref[:, 0:1, :], 0)
    dgain = jnp.sum(gathered_ref[:, 1:2, :], 0)
    slope = scale * gain
    return (slope * dz - slope * dbias / total - unit * (slope * dgain / total), dgain, dbias)


def back_two_kernel(
    place_ref, cumulative_ref, dz_ref, unit_ref, stats2_ref, back_ref, gain2_ref, target_ref,
    kernel_ref, hidden_ref, y1_ref, stats1_ref, gain1_ref, bias1_ref,
    dkernel_ref, dz1_ref, head_ref, tail_ref, stats_ref, dgain_ref, dbias_ref,
    halves, dfield,
):
    live, count = place_ref[1], stats1_ref.shape[0]
    total = cumulative_ref[count].astype(F32)
    width = kernel_ref.shape[2]
    _, scale2 = norm_stats(stats2_ref, cumulative_ref)
    dy, dgain, dbias = norm_back(
        dz_ref[...], unit_ref[...], scale2, gain2_ref[...], back_ref, total
    )
    dgain_ref[...] = dgain
    dbias_ref[...] = dbias
    high, low = split(dy)
    halves[:, :width] = high
    halves[:, width:] = low
    high, low = split(hidden_ref[...].T)
    scatter_conv(
        halves, target_ref, kernel_ref, jnp.concatenate([high, low], 0), dkernel_ref, dfield
    )
    mean1, scale1 = norm_stats(stats1_ref, cumulative_ref)
    mask = row_mask(y1_ref.shape[0], live)
    unit1 = (y1_ref[...] - mean1) * scale1
    dz1 = jnp.where(
        mask, dfield[...] * silu_slope(unit1 * gain1_ref[...] + bias1_ref[...]), 0.0
    )
    dz1_ref[...] = dz1
    share(stats_ref, jnp.sum(dz1, 0, keepdims=True), jnp.sum(dz1 * unit1, 0, keepdims=True))
    edges(head_ref, tail_ref, dz1_ref, live)


def back_one_kernel(
    place_ref, cumulative_ref, dz_ref, before_ref, after_ref, y_ref, y_before_ref, y_after_ref,
    stats_ref, back_ref, gain_ref, target_ref, kernel_ref, x_ref, dpre_ref,
    dkernel_ref, dx_ref, dgain_ref, dbias_ref,
    halves, dfield, ext,
):
    live, count = place_ref[1], stats_ref.shape[0]
    total = cumulative_ref[count].astype(F32)
    width = kernel_ref.shape[2]
    rows = x_ref.shape[0]
    mean, scale = norm_stats(stats_ref, cumulative_ref)

    def part(dz, y):
        return norm_back(dz, (y - mean) * scale, scale, gain_ref[...], back_ref, total)

    dy, dgain, dbias = part(dz_ref[...], y_ref[...])
    dgain_ref[...] = dgain
    dbias_ref[...] = dbias
    place(
        ext,
        part(before_ref[...], y_before_ref[...])[0],
        dy,
        part(after_ref[...], y_after_ref[...])[0],
        live,
    )
    high, low = split(ext[...])
    halves[:, :width] = high
    halves[:, width:] = low
    high, low = split(x_ref[...].T)
    scatter_conv(
        halves, target_ref, kernel_ref, jnp.concatenate([high, low], 0), dkernel_ref, dfield
    )
    dx_ref[...] = dfield[...] + jnp.where(
        row_mask(rows, live), dpre_ref[HALO : HALO + rows, :], 0.0
    )


def run(body, scalars, arrays, outs, scratch):
    return pl.pallas_call(
        body,
        in_specs=[pl.BlockSpec(memory_space=pltpu.SMEM)] * len(scalars)
        + [pl.BlockSpec(memory_space=pltpu.VMEM)] * len(arrays),
        out_specs=[pl.BlockSpec(memory_space=pltpu.VMEM)] * len(outs),
        out_shape=[jax.ShapeDtypeStruct(shape, F32) for shape in outs],
        scratch_shapes=scratch,
        compiler_params=pltpu.CompilerParams(vmem_limit_bytes=56 * 2**20),
    )(*scalars, *arrays)


def all_reduce(parts, orders, rank, count):
    def swap(piece, bit):
        return lax.ppermute(piece, "vox", [(i, i ^ bit) for i in range(count)])

    pieces = list(parts)
    for stage in range(len(orders[0])):
        sent, kept = [], []
        for piece, order in zip(pieces, orders):
            up = (rank // order[stage]) % 2
            half = piece.shape[0] // 2
            sent.append(lax.dynamic_slice_in_dim(piece, (1 - up) * half, half, 0))
            kept.append(lax.dynamic_slice_in_dim(piece, up * half, half, 0))
        got = [swap(piece, order[stage]) for piece, order in zip(sent, orders)]
        pieces = [a + b for a, b in zip(kept, got)]
    for stage in reversed(range(len(orders[0]))):
        got = [swap(piece, order[stage]) for piece, order in zip(pieces, orders)]
        wider = []
        for piece, other, order in zip(pieces, got, orders):
            up = (rank // order[stage]) % 2
            wider.append(
                jnp.concatenate([jnp.where(up, other, piece), jnp.where(up, piece, other)], 0)
            )
        pieces = wider
    return pieces


def reduce_kernels(one, two, rank, count):
    shape = one.shape
    bits = [1 << i for i in range(count.bit_length() - 1)]
    first, rest = bits[0], bits[1:]
    ways = 3
    orders = [(first, *rest[w % len(rest) :], *rest[: w % len(rest)]) for w in range(ways)]
    flat = jnp.concatenate([one.reshape(-1, 8, shape[2]), two.reshape(-1, 8, shape[2])], 0)
    tiles = flat.shape[0]
    unit = ways * count
    padded = -(-tiles // unit) * unit
    if padded > tiles:
        flat = jnp.concatenate([flat, jnp.zeros((padded - tiles, 8, shape[2]), F32)], 0)
    size = padded // ways
    parts = [flat[w * size : (w + 1) * size] for w in range(ways)]
    flat = jnp.concatenate(all_reduce(parts, orders, rank, count), 0)
    half = tiles // 2
    return (flat[:half].reshape(shape), flat[half:tiles].reshape(shape))


def per_device(
    features,
    kernel_one,
    gain_one,
    bias_one,
    kernel_two,
    gain_two,
    bias_two,
    cotangent,
    cumulative,
    neighbours,
):
    rank = lax.axis_index("vox")
    count = cumulative.shape[0] - 1
    live = cumulative[rank + 1] - cumulative[rank]
    rows, width = features.shape
    offsets = neighbours.shape[0]
    scalars = jnp.stack([rank, live]).astype(jnp.int32)
    gain_one, bias_one = gain_one[None], bias_one[None]
    gain_two, bias_two = gain_two[None], bias_two[None]

    def exchange(head, tail):
        before = lax.ppermute(tail, "vox", [(i, i + 1) for i in range(count - 1)])
        after = lax.ppermute(head, "vox", [(i + 1, i) for i in range(count - 1)])
        return (before, after)

    def spread(stats):
        return lax.all_to_all(stats, "vox", 0, 0)

    def pack(start):
        def rows_at(array):
            return lax.dynamic_slice_in_dim(array, start, HALO, 0)

        entries = lax.dynamic_slice_in_dim(neighbours, start, HALO, 1).astype(F32)
        return jnp.concatenate([rows_at(features), rows_at(cotangent), entries], 0)

    before, after = exchange(pack(0), pack(live - HALO))

    def entries(packed):
        return packed[2 * HALO :].astype(jnp.int32)

    own = jnp.where((neighbours >= HALO) & (neighbours < HALO + rows), neighbours - HALO, -1)
    from_before = entries(before) - (HALO + rows)
    from_before = jnp.where((from_before >= 0) & (rank > 0), from_before, -1)
    from_after = entries(after)
    from_after = jnp.where(
        (from_after >= 0) & (from_after < HALO) & (rank < count - 1),
        from_after + live - HALO,
        -1,
    )
    target = jnp.concatenate([from_before, own, jnp.full((offsets, HALO), -1, jnp.int32)], 1)
    target = lax.dynamic_update_slice(target, from_after, (0, live + HALO))

    ext_shape = (rows + 2 * HALO, width)
    stats_shape = (count, 2, width)
    edge = (HALO, width)
    vector = (1, width)
    conv_scratch = [
        pltpu.VMEM(ext_shape, F32),
        pltpu.VMEM((ext_shape[0], 2 * width), BF16),
        pltpu.VMEM((offsets, rows, 2 * width), BF16),
        pltpu.VMEM((-(-offsets // 8) * 8, rows), jnp.int32),
    ]
    back_scratch = [
        pltpu.VMEM((ext_shape[0], 2 * width), BF16),
        pltpu.VMEM((rows, width), F32),
    ]

    y1, head, tail, stats = run(
        first_kernel,
        (scalars,),
        (features, before[:HALO], after[:HALO], neighbours, kernel_one),
        ((rows, width), edge, edge, stats_shape),
        conv_scratch,
    )
    y1_before, y1_after = exchange(head, tail)
    stats1 = spread(stats)
    y2, head, tail, stats, hidden = run(
        second_kernel,
        (scalars, cumulative),
        (y1, y1_before, y1_after, stats1, gain_one, bias_one, neighbours, kernel_two),
        ((rows, width), edge, edge, stats_shape, (rows, width)),
        conv_scratch,
    )
    y2_before, y2_after = exchange(head, tail)
    stats2 = spread(stats)
    output, dz2, unit2, stats = run(
        middle_kernel,
        (scalars, cumulative),
        (y2, y2_before, y2_after, stats2, gain_two, bias_two, features, before, after, cotangent),
        ((rows, width), ext_shape, ext_shape, stats_shape),
        [],
    )
    back2 = spread(stats)
    dkernel_two, dz1, head, tail, stats, dgain_two, dbias_two = run(
        back_two_kernel,
        (scalars, cumulative),
        (
            dz2, unit2, stats2, back2, gain_two, target, kernel_two, hidden, y1, stats1, gain_one,
            bias_one,
        ),
        ((offsets, width, width), (rows, width), edge, edge, stats_shape, vector, vector),
        back_scratch,
    )
    dz_before, dz_after = exchange(head, tail)
    back1 = spread(stats)
    dkernel_one, dx, dgain_one, dbias_one = run(
        back_one_kernel,
        (scalars, cumulative),
        (
            dz1, dz_before, dz_after, y1, y1_before, y1_after, stats1, back1, gain_one, target,
            kernel_one, features, dz2,
        ),
        ((offsets, width, width), (rows, width), vector, vector),
        back_scratch + [pltpu.VMEM(ext_shape, F32)],
    )
    dkernel_one, dkernel_two = reduce_kernels(dkernel_one, dkernel_two, rank, count)
    return (
        output,
        dx,
        dkernel_one,
        dkernel_two,
        dgain_one[0],
        dbias_one[0],
        dgain_two[0],
        dbias_two[0],
    )


def solution(mesh):
    return jax.shard_map(
        per_device,
        mesh=mesh,
        in_specs=(
            P("vox", None),
            P(),
            P(),
            P(),
            P(),
            P(),
            P(),
            P("vox", None),
            P(),
            P(None, "vox"),
        ),
        out_specs=(P("vox", None), P("vox", None), P(), P(), P(), P(), P(), P()),
        check_vma=False,
    )
```

```python
import functools

import jax
import jax.numpy as jnp
from jax import lax
from jax.experimental import pallas as pl
from jax.experimental.pallas import tpu as pltpu
from jax.sharding import PartitionSpec as P

HALO = 128
BLOCK = 256
SPAN = BLOCK + 2 * HALO
EPS = 1e-05
CHUNKS = (0.0, 0.4, 0.75, 1.0)
F32 = jnp.float32
BF16 = jnp.bfloat16


def split(values):
    high = values.astype(BF16)
    low = (values - high.astype(F32)).astype(BF16)
    return (high, low)


def silu_slope(values):
    sigma = jax.nn.sigmoid(values)
    return sigma * (1.0 + values * (1.0 - sigma))


def position(cumulative_ref):
    rank = lax.axis_index("vox")
    return (rank, cumulative_ref[rank + 1] - cumulative_ref[rank], rank % 2 == 0)


def sides(first, second, even):
    return (jnp.where(even, second, first), jnp.where(even, first, second))


def row_mask(rows, live):
    return lax.broadcasted_iota(jnp.int32, (rows, 1), 0) < live


def place(ref, before, own, after, live):
    rows = own.shape[0]
    ref[:HALO, :] = before
    ref[HALO : HALO + rows, :] = own
    ref[HALO + rows :, :] = jnp.zeros((HALO, own.shape[1]), F32)
    ref[pl.ds(HALO + live, HALO), :] = after


def one_hot(index, rows, axis):
    shape = (rows, SPAN) if axis == 1 else (rows, index.shape[1])
    return (index == lax.broadcasted_iota(jnp.int32, shape, axis)).astype(F32).astype(BF16)


def gather_conv(ext, index_ref, kernel_ref, stash_ref, matrices, taken, halves, turned, sems, live):
    offsets, width = kernel_ref.shape[0], kernel_ref.shape[2]
    rows = index_ref.shape[1]
    blocks = rows // BLOCK
    fetch = pltpu.make_async_copy(kernel_ref, matrices, sems.at[blocks])
    fetch.start()
    high, low = split(ext[...])
    halves[:, :width] = high
    halves[:, width:] = low
    index = index_ref[...]
    index = jnp.where(index >= HALO + rows, index - rows + live, index)
    turned[:offsets, :] = index
    turned[offsets:, :] = jnp.full((turned.shape[0] - offsets, rows), -1, jnp.int32)
    stashes = []
    for b in range(blocks):
        window = halves[BLOCK * b : BLOCK * b + SPAN, :]
        columns = jnp.concatenate(
            [
                turned[:, BLOCK * b + HALO * h : BLOCK * b + HALO * (h + 1)].T
                for h in range(BLOCK // HALO)
            ],
            0,
        ) - (BLOCK * b)
        for k in range(offsets):
            hit = one_hot(columns[:, k : k + 1], BLOCK, 1)
            taken[k, BLOCK * b : BLOCK * (b + 1), :] = jnp.dot(
                hit, window, preferred_element_type=F32
            ).astype(BF16)
        part = (slice(None), pl.ds(BLOCK * b, BLOCK), slice(None))
        stashes.append(pltpu.make_async_copy(taken.at[part], stash_ref.at[part], sems.at[b]))
        stashes[b].start()
    fetch.wait()
    total = jnp.zeros((rows, 2 * width), F32)
    for k in range(offsets):
        both = jnp.concatenate(split(matrices[k]), 1)
        total = total + jnp.dot(
            taken[k], jnp.concatenate([both, both], 0), preferred_element_type=F32
        )
    for stash in stashes:
        stash.wait()
    return total[:, :width] + total[:, width:]


def scatter_conv(halves, target_ref, kernel_ref, blocks):
    offsets, width = kernel_ref.shape[0], kernel_ref.shape[2]
    total = jnp.zeros((len(blocks) * BLOCK, 2 * width), F32)
    for k in range(offsets):
        spread = []
        for b in blocks:
            index = target_ref[k : k + 1, BLOCK * b : BLOCK * b + SPAN] - BLOCK * b
            window = halves[BLOCK * b : BLOCK * b + SPAN, :]
            got = jnp.dot(one_hot(index, BLOCK, 0), window, preferred_element_type=F32)
            spread.append(jnp.concatenate(split(got[:, :width] + got[:, width:]), 1))
        tall = jnp.concatenate(split(kernel_ref[k]), 0)
        total = total + lax.dot_general(
            jnp.concatenate(spread, 0),
            jnp.concatenate([tall, tall], 1),
            (((1,), (1,)), ((), ())),
            preferred_element_type=F32,
        )
    return total[:, :width] + total[:, width:]


def kernel_grads(make_dy, stash_ref, taken, sems, store):
    offsets, width = taken.shape[0], taken.shape[2] // 2
    ends = [round(offsets * e) for e in CHUNKS]
    fetches = []
    for c, (start, end) in enumerate(zip(ends, ends[1:])):
        part = pl.ds(start, end - start)
        fetches.append(pltpu.make_async_copy(stash_ref.at[part], taken.at[part], sems.at[c]))
        fetches[c].start()
    turned = jnp.concatenate(split(make_dy().T), 0)
    for c, (start, end) in enumerate(zip(ends, ends[1:])):
        fetches[c].wait()
        for k in range(start, end):
            outer = jnp.dot(turned, taken[k], preferred_element_type=F32)
            outer = outer[:, :width] + outer[:, width:]
            store(k, (outer[:width] + outer[width:]).T)


class Ring:
    def __init__(self, count, tiles):
        bits = list(range(1, count.bit_length() - 1))
        self.orders = [bits, bits[1::-1] + bits[:1:-1], bits[2:] + bits[:2]]
        self.chips = count // 2
        self.tiles = tiles
        self.size = -(-tiles // (self.chips * len(self.orders)))
        self.part = self.chips * self.size
        self.padded = self.part * len(self.orders)

    def codes(self, rank):
        return [sum(((rank >> bit) & 1) << (len(order) - 1 - s) for s, bit in enumerate(order)) for order in self.orders]

    def store(self, ref, codes, first, value):
        for j in range(value.shape[0] // 8):
            part, tile = divmod(first + j, self.part)
            block, tile = divmod(tile, self.size)
            at = part * self.part + (block ^ codes[part]) * self.size + tile
            ref[at] = value[8 * j : 8 * (j + 1), :]


def norm_stats(gathered_ref, cumulative_ref):
    count = gathered_ref.shape[0]
    total = cumulative_ref[count].astype(F32)
    mean = jnp.sum(gathered_ref[:, 0:1, :], 0) / total

    def step(d, spread):
        live = (cumulative_ref[d + 1] - cumulative_ref[d]).astype(F32)
        own = gathered_ref[d, 0:1, :] / live - mean
        return spread + gathered_ref[d, 1:2, :] + live * own * own

    spread = lax.fori_loop(0, count, step, jnp.zeros_like(mean))
    return (mean, lax.rsqrt(spread / total + EPS))


def share(stats_ref, first, second):
    both = jnp.concatenate([first, second], 0)
    stats_ref[...] = jnp.broadcast_to(both[None], stats_ref.shape)


def conv_stats(y, mask, live, stats_ref):
    first = jnp.sum(y, 0, keepdims=True)
    centred = jnp.where(mask, y - first / live.astype(F32), 0.0)
    share(stats_ref, first, jnp.sum(centred * centred, 0, keepdims=True))


def edges(first_ref, second_ref, ref, live, even):
    first_ref[...] = ref[pl.ds(jnp.where(even, live - HALO, 0), HALO), :]
    second_ref[...] = ref[pl.ds(jnp.where(even, 0, live - HALO), HALO), :]


def targets(target_ref, index_ref, before, after, live, rank, count, spread):
    rows = index_ref.shape[1]
    offsets = index_ref.shape[0]
    own = index_ref[...]
    own = jnp.where((own >= HALO) & (own < HALO + rows), own - HALO, -1)
    before = before.astype(jnp.int32) - (HALO + rows)
    before = jnp.where((before >= 0) & (rank > 0), before, -1)
    after = after.astype(jnp.int32)
    after = jnp.where(
        (after >= 0) & (after < HALO) & (rank < count - 1), after + live - HALO, -1
    )
    fill = jnp.full((target_ref.shape[0] - offsets, HALO), -1, jnp.int32)

    def turn(block):
        return jnp.concatenate([block, fill], 0).T

    spread[:HALO, :] = turn(before)
    for j in range(rows // HALO):
        spread[HALO * (j + 1) : HALO * (j + 2), :] = turn(own[:, HALO * j : HALO * (j + 1)])
    spread[HALO + rows :, :] = jnp.full((HALO, target_ref.shape[0]), -1, jnp.int32)
    spread[pl.ds(HALO + live, HALO), :] = turn(after)
    for j in range(target_ref.shape[1] // HALO):
        target_ref[:, HALO * j : HALO * (j + 1)] = spread[HALO * j : HALO * (j + 1), :].T


def first_kernel(
    cumulative_ref, x_ref, pack1_ref, pack2_ref, index_ref, kernel_ref,
    y_ref, swap1_ref, swap2_ref, stats_ref, stash_ref,
    ext, *scratch,
):
    _, live, even = position(cumulative_ref)
    before, after = sides(pack1_ref[:HALO, :], pack2_ref[:HALO, :], even)
    place(ext, before, x_ref[...], after, live)
    y = gather_conv(ext, index_ref, kernel_ref, stash_ref, *scratch, live)
    y_ref[...] = y
    conv_stats(y, row_mask(y.shape[0], live), live, stats_ref)
    edges(swap1_ref, swap2_ref, y_ref, live, even)


def second_kernel(
    cumulative_ref, y1_ref, y1_swap1_ref, y1_swap2_ref, gathered_ref, gain_ref, bias_ref,
    index_ref, pack1_ref, pack2_ref, kernel_ref,
    y_ref, swap1_ref, swap2_ref, stats_ref, stash_ref, target_ref,
    spread, ext, *scratch,
):
    rank, live, even = position(cumulative_ref)
    count = gathered_ref.shape[0]
    mean, scale = norm_stats(gathered_ref, cumulative_ref)
    rows = y1_ref.shape[0]
    mask = row_mask(rows, live)

    def act(y):
        a = (y - mean) * scale * gain_ref[...] + bias_ref[...]
        return a * jax.nn.sigmoid(a)

    own = jnp.where(mask, act(y1_ref[...]), 0.0)
    before, after = sides(y1_swap1_ref[...], y1_swap2_ref[...], even)
    before = jnp.where(rank > 0, act(before), 0.0)
    after = jnp.where(rank < count - 1, act(after), 0.0)
    place(ext, before, own, after, live)
    before, after = sides(pack1_ref[2 * HALO :, :], pack2_ref[2 * HALO :, :], even)
    targets(target_ref, index_ref, before, after, live, rank, count, spread)
    y = gather_conv(ext, index_ref, kernel_ref, stash_ref, *scratch, live)
    y_ref[...] = y
    conv_stats(y, mask, live, stats_ref)
    edges(swap1_ref, swap2_ref, y_ref, live, even)


def middle_kernel(
    cumulative_ref, y_ref, y_swap1_ref, y_swap2_ref, gathered_ref, gain_ref, bias_ref,
    x_ref, pack1_ref, pack2_ref, cotangent_ref,
    out_ref, dz_ref, unit_ref, stats_ref,
):
    _, live, even = position(cumulative_ref)
    mean, scale = norm_stats(gathered_ref, cumulative_ref)
    mask = row_mask(x_ref.shape[0], live)

    def part(y, x, cotangent):
        unit = (y - mean) * scale
        pre = unit * gain_ref[...] + bias_ref[...] + x
        return (unit, pre, cotangent * silu_slope(pre))

    unit, pre, dz = part(y_ref[...], x_ref[...], cotangent_ref[...])
    dz = jnp.where(mask, dz, 0.0)
    out_ref[...] = jnp.where(mask, pre * jax.nn.sigmoid(pre), 0.0)
    share(
        stats_ref, jnp.sum(dz, 0, keepdims=True), jnp.sum(dz * unit, 0, keepdims=True)
    )
    y_before, y_after = sides(y_swap1_ref[...], y_swap2_ref[...], even)
    before, after = sides(pack1_ref[: 2 * HALO, :], pack2_ref[: 2 * HALO, :], even)
    unit_b, _, dz_b = part(y_before, before[:HALO], before[HALO:])
    unit_a, _, dz_a = part(y_after, after[:HALO], after[HALO:])
    place(dz_ref, dz_b, dz, dz_a, live)
    place(unit_ref, unit_b, unit, unit_a, live)


def norm_back(dz, unit, scale, gain, gathered_ref, total):
    dbias = jnp.sum(gathered_ref[:, 0:1, :], 0)
    dgain = jnp.sum(gathered_ref[:, 1:2, :], 0)
    slope = scale * gain
    return (slope * dz - slope * dbias / total - unit * (slope * dgain / total), dgain, dbias)


def back_two_kernel(
    cumulative_ref, dz_ref, unit_ref, stats2_ref, back_ref, gain2_ref, target_ref,
    y1_ref, stats1_ref, gain1_ref, bias1_ref, kernel_ref,
    dy_ref, dz1_ref, swap1_ref, swap2_ref, stats_ref, dgain_ref, dbias_ref,
    halves,
):
    _, live, even = position(cumulative_ref)
    count = stats1_ref.shape[0]
    total = cumulative_ref[count].astype(F32)
    rows, width = y1_ref.shape
    _, scale2 = norm_stats(stats2_ref, cumulative_ref)
    dy, dgain, dbias = norm_back(
        dz_ref[...], unit_ref[...], scale2, gain2_ref[...], back_ref, total
    )
    dgain_ref[...] = dgain
    dbias_ref[...] = dbias
    dy_ref[...] = dy[HALO : HALO + rows]
    high, low = split(dy)
    halves[:, :width] = high
    halves[:, width:] = low
    dhidden = scatter_conv(halves, target_ref, kernel_ref, range(rows // BLOCK))
    mean1, scale1 = norm_stats(stats1_ref, cumulative_ref)
    unit1 = (y1_ref[...] - mean1) * scale1
    slope = silu_slope(unit1 * gain1_ref[...] + bias1_ref[...])
    dz1 = jnp.where(row_mask(rows, live), dhidden * slope, 0.0)
    dz1_ref[...] = dz1
    share(stats_ref, jnp.sum(dz1, 0, keepdims=True), jnp.sum(dz1 * unit1, 0, keepdims=True))
    edges(swap1_ref, swap2_ref, dz1_ref, live, even)


def grad_two_kernel(ring, dy_ref, stash_ref, grad_ref, taken, sems):
    codes = ring.codes(lax.axis_index("vox"))

    def store(k, value):
        ring.store(grad_ref, codes, k * (value.shape[0] // 8), value)

    kernel_grads(lambda: dy_ref[...], stash_ref, taken, sems, store)


def grad_one_kernel(
    ring,
    cumulative_ref, dz_ref, swap1_ref, swap2_ref, y_ref, y_swap1_ref, y_swap2_ref,
    stats_ref, back_ref, gain_ref, two_ref, stash_ref,
    keep_ref, give_ref, halves_ref, dgain_ref, dbias_ref,
    ext, grad, taken, sems,
):
    rank, live, even = position(cumulative_ref)
    total = cumulative_ref[stats_ref.shape[0]].astype(F32)
    width = y_ref.shape[1]
    codes = ring.codes(rank)

    def make_dy():
        mean, scale = norm_stats(stats_ref, cumulative_ref)

        def part(dz, y):
            return norm_back(dz, (y - mean) * scale, scale, gain_ref[...], back_ref, total)

        dz_before, dz_after = sides(swap1_ref[...], swap2_ref[...], even)
        y_before, y_after = sides(y_swap1_ref[...], y_swap2_ref[...], even)
        dy, dgain, dbias = part(dz_ref[...], y_ref[...])
        dgain_ref[...] = dgain
        dbias_ref[...] = dbias
        place(ext, part(dz_before, y_before)[0], dy, part(dz_after, y_after)[0], live)
        high, low = split(ext[...])
        halves_ref[:, :width] = high
        halves_ref[:, width:] = low
        return dy

    def store(k, value):
        ring.store(grad, codes, k * (value.shape[0] // 8), value)

    kernel_grads(make_dy, stash_ref, taken, sems, store)
    keep_ref[...] = jnp.where(even, two_ref[...], grad[...])
    give_ref[...] = jnp.where(even, grad[...], two_ref[...])


def back_one_kernel(
    block, cumulative_ref, halves_ref, target_ref, dpre_ref, kernel_ref, *refs
):
    dx_ref, zero_ref, result, sem = refs[-4:]
    _, live, _ = position(cumulative_ref)
    rows = BLOCK * block
    dx = scatter_conv(halves_ref, target_ref, kernel_ref, (block,))
    dpre = dpre_ref[HALO + rows : HALO + rows + BLOCK, :]
    result[...] = dx + jnp.where(row_mask(BLOCK, live - rows), dpre, 0.0)
    store = pltpu.make_async_copy(result, dx_ref.at[pl.ds(rows, BLOCK)], sem)
    store.start()
    zero_ref[...] = jnp.zeros_like(zero_ref)
    store.wait()


def finish_kernel(ring, *refs):
    count = len(ring.orders)
    low, high, low_other, high_other = (refs[i * count : (i + 1) * count] for i in range(4))
    one_ref, two_ref, sems = refs[4 * count :]
    rank = lax.axis_index("vox")
    codes = ring.codes(rank)
    half = ring.chips // 2

    def spread(pieces, ref, sem):
        for part, halves in enumerate(zip(*pieces)):
            for block in range(ring.chips):
                at = part * ring.part + (block ^ codes[part]) * ring.size
                pltpu.make_async_copy(
                    halves[block // half].at[pl.ds(block % half * ring.size, ring.size)],
                    ref.at[pl.ds(at, ring.size)],
                    sem,
                ).start()

    def finish(own_ref, other_ref):
        spread((low, high), own_ref, sems.at[0])
        spread((low_other, high_other), other_ref, sems.at[1])
        for i, ref in enumerate((own_ref, other_ref)):
            pltpu.make_async_copy(ref, ref, sems.at[i]).wait()

    @pl.when(rank % 2 == 0)
    def _():
        finish(two_ref, one_ref)

    @pl.when(rank % 2 == 1)
    def _():
        finish(one_ref, two_ref)


def run(body, cumulative, arrays, outs, scratch, flops=0, limit=28, aliases=None):
    plain = pl.BlockSpec(memory_space=pltpu.VMEM)
    there = pl.BlockSpec(memory_space=pltpu.MemorySpace.HBM)
    shapes, out_specs = [], []
    for out in outs:
        if out[0] == "near":
            shapes.append(pltpu.VMEM(*out[1:]))
            out_specs.append(plain)
        elif out[0] == "far":
            shapes.append(pltpu.MemorySpace.HBM(*out[1:]))
            out_specs.append(there)
        else:
            shapes.append(jax.ShapeDtypeStruct(out, F32))
            out_specs.append(plain)
    any_space = pl.BlockSpec(memory_space=pl.ANY)
    operands, specs = [], []
    if cumulative is not None:
        operands.append(cumulative)
        specs.append(pl.BlockSpec(memory_space=pltpu.SMEM))
    for array in arrays:
        how, array = array if isinstance(array, tuple) else ("near", array)
        specs.append({"near": plain, "here": plain, "far": there, "any": any_space}[how])
        if how in ("near", "far"):
            space = pltpu.VMEM if how == "near" else pltpu.MemorySpace.HBM
            array = pltpu.with_memory_space_constraint(array, space)
        operands.append(array)
    return pl.pallas_call(
        body,
        in_specs=specs,
        out_specs=out_specs,
        out_shape=shapes,
        scratch_shapes=scratch,
        input_output_aliases=aliases or {},
        cost_estimate=pl.CostEstimate(flops=flops, bytes_accessed=2**20, transcendentals=0),
        compiler_params=pltpu.CompilerParams(vmem_limit_bytes=limit * 2**20),
    )(*operands)


def sum_chips(ring, pairs, swap_chips, swap_cores, beside, zero):
    stages = len(ring.orders[0])
    for stage in range(stages):
        wider = []
        for (a, b), order in zip(pairs, ring.orders):
            half = a.shape[0] // 2
            sent = a[half:] + b[half:]
            if zero is not None:
                sent = sent + zero
            wider.append((a[:half] + b[:half], swap_chips(sent, order[stage])))
        pairs = wider
        zero = beside(sent)
    pieces = [a + b for a, b in pairs]
    for stage in reversed(range(1, stages)):
        pieces = [
            jnp.concatenate([piece, swap_chips(piece, order[stage])], 0)
            for piece, order in zip(pieces, ring.orders)
        ]
    highs = [swap_chips(piece, order[0]) for piece, order in zip(pieces, ring.orders)]
    return (*pieces, *highs, *map(swap_cores, pieces), *map(swap_cores, highs))


def per_device(
    features,
    kernel_one,
    gain_one,
    bias_one,
    kernel_two,
    gain_two,
    bias_two,
    cotangent,
    cumulative,
    neighbours,
):
    rank = lax.axis_index("vox")
    count = cumulative.shape[0] - 1
    ends = lax.dynamic_slice(cumulative, (rank,), (2,), allow_negative_indices=False)
    tail = ends[1] - ends[0] - HALO
    rows, width = features.shape
    offsets = neighbours.shape[0]
    even = rank % 2 == 0
    gain_one, bias_one = gain_one[None], bias_one[None]
    gain_two, bias_two = gain_two[None], bias_two[None]

    def swap(first, second):
        within = [(i, i ^ 1) for i in range(count)]
        across = [(i, i + 1) for i in range(1, count - 1, 2)]
        across = across + [(j, i) for i, j in across]
        return (lax.ppermute(first, "vox", within), lax.ppermute(second, "vox", across))

    def spread(stats):
        return lax.all_to_all(stats, "vox", 0, 0)

    def pack(start):
        def part(array, shape, where):
            return lax.dynamic_slice(array, where, shape, allow_negative_indices=False)

        zero = jnp.zeros_like(start)
        return jnp.concatenate(
            [
                part(features, (HALO, width), (start, zero)),
                part(cotangent, (HALO, width), (start, zero)),
                part(neighbours, (offsets, HALO), (zero, start)).astype(F32),
            ],
            0,
        )

    packs = swap(pack(jnp.where(even, tail, 0)), pack(jnp.where(even, 0, tail)))

    ext_shape = (rows + 2 * HALO, width)
    stats_shape = (count, 2, width)
    edge = (HALO, width)
    vector = (1, width)
    turned_rows = -(-offsets // 8) * 8
    taken = (offsets, rows, 2 * width)
    halves = (ext_shape[0], 2 * width)
    conv_scratch = [
        pltpu.VMEM(ext_shape, F32),
        pltpu.VMEM((offsets, width, width), F32),
        pltpu.VMEM(taken, BF16),
        pltpu.VMEM(halves, BF16),
        pltpu.VMEM((turned_rows, rows), jnp.int32),
        pltpu.SemaphoreType.DMA((rows // BLOCK + 1,)),
    ]
    grad_scratch = [pltpu.VMEM(taken, BF16), pltpu.SemaphoreType.DMA((len(CHUNKS) - 1,))]
    ring = Ring(count, offsets * width // 8)
    grad = (ring.padded, 8, width)
    work = 2 * offsets * rows * width * width * 4

    def move(piece, pairs):
        return lax.ppermute(piece, "vox", pairs)

    def near(shape, kind=F32):
        return ("near", shape, kind)

    y1, swap1, swap2, stats, stash1 = run(
        first_kernel,
        cumulative,
        (("here", features), *packs, ("here", neighbours), ("far", kernel_one)),
        (near((rows, width)), edge, edge, stats_shape, ("far", taken, BF16)),
        conv_scratch,
        flops=3 * work,
    )
    y1_edges = swap(swap1, swap2)
    stats1 = spread(stats)
    y2, swap1, swap2, stats, stash2, target = run(
        second_kernel,
        cumulative,
        (y1, *y1_edges, stats1, gain_one, bias_one, neighbours, *packs, ("far", kernel_two)),
        (
            near((rows, width)), edge, edge, stats_shape, ("far", taken, BF16),
            near((turned_rows, ext_shape[0]), jnp.int32),
        ),
        [pltpu.VMEM((ext_shape[0], turned_rows), jnp.int32), *conv_scratch],
        flops=3 * work,
    )
    y2_edges = swap(swap1, swap2)
    stats2 = spread(stats)
    output, dz2, unit2, stats = run(
        middle_kernel,
        cumulative,
        (y2, *y2_edges, stats2, gain_two, bias_two, features, *packs, cotangent),
        ((rows, width), near(ext_shape), near(ext_shape), stats_shape),
        [],
    )
    back2 = spread(stats)
    dy2, dz1, swap1, swap2, stats, dgain_two, dbias_two = run(
        back_two_kernel,
        cumulative,
        (
            dz2, unit2, stats2, back2, gain_two, target, y1, stats1, gain_one, bias_one,
            kernel_two,
        ),
        (near((rows, width)), near((rows, width)), edge, edge, stats_shape, vector, vector),
        [pltpu.VMEM(halves, BF16)],
        flops=3 * work,
    )
    dz_edges = swap(swap1, swap2)
    back1 = spread(stats)
    (two,) = run(
        functools.partial(grad_two_kernel, ring),
        None,
        (dy2, ("far", stash2)),
        (near(grad),),
        grad_scratch,
        flops=work,
    )
    keep, give, halves_one, dgain_one, dbias_one = run(
        functools.partial(grad_one_kernel, ring),
        cumulative,
        (
            dz1, *dz_edges, y1, *y1_edges, stats1, back1, gain_one, two, ("far", stash1),
        ),
        (grad, grad, near(halves, BF16), vector, vector),
        [pltpu.VMEM(ext_shape, F32), pltpu.VMEM(grad, F32), *grad_scratch],
        flops=work,
    )
    theirs = move(give, [(i, i ^ 1) for i in range(count)])
    dx = None
    blocks = list(range(rows // BLOCK))

    def beside(sent):
        nonlocal dx
        if not blocks:
            return None
        block = blocks.pop(0)
        arrays = (halves_one, target, dz2, kernel_one, ("any", sent))
        dx, zero = run(
            functools.partial(back_one_kernel, block),
            cumulative,
            arrays if dx is None else (*arrays, ("far", dx)),
            (("far", (rows, width), F32), (8, width)),
            [pltpu.VMEM((BLOCK, width), F32), pltpu.SemaphoreType.DMA],
            flops=3 * work // (rows // BLOCK),
            aliases=None if dx is None else {len(arrays) + 1: 0},
        )
        return zero

    def part(array, w):
        return array[w * ring.part : (w + 1) * ring.part]

    sums = sum_chips(
        ring,
        [(part(keep, w), part(theirs, w)) for w in range(len(ring.orders))],
        lambda piece, bit: move(piece, [(i, i ^ (1 << bit)) for i in range(count)]),
        lambda piece: move(piece, [(i, i ^ 1) for i in range(count)]),
        beside,
        beside(give),
    )
    while blocks:
        beside(give)
    grads = run(
        functools.partial(finish_kernel, ring),
        None,
        [("any", piece) for piece in sums],
        (("far", grad, F32), ("far", grad, F32)),
        [pltpu.SemaphoreType.DMA((2,))],
    )
    dkernel_one, dkernel_two = (
        array[: ring.tiles].reshape(offsets, width, width) for array in grads
    )
    return (
        output,
        dx,
        dkernel_one,
        dkernel_two,
        dgain_one[0],
        dbias_one[0],
        dgain_two[0],
        dbias_two[0],
    )


def solution(mesh):
    return jax.shard_map(
        per_device,
        mesh=mesh,
        in_specs=(
            P("vox", None),
            P(),
            P(),
            P(),
            P(),
            P(),
            P(),
            P("vox", None),
            P(),
            P(None, "vox"),
        ),
        out_specs=(P("vox", None), P("vox", None), P(), P(), P(), P(), P(), P()),
        check_vma=False,
    )
```

```python
import functools

import jax
import jax.numpy as jnp
from jax import lax
from jax.experimental import pallas as pl
from jax.experimental.pallas import tpu as pltpu
from jax.sharding import PartitionSpec as P

HALO = 128
BLOCK = 256
SPAN = BLOCK + 2 * HALO
EPS = 1e-05
SHARE = 9
BESIDE = ((0,), (1,))
LATE = 2
CHUNKS = (0.0, 0.4, 0.75, 1.0)
F32 = jnp.float32
BF16 = jnp.bfloat16


def split(values):
    high = values.astype(BF16)
    low = (values - high.astype(F32)).astype(BF16)
    return (high, low)


def silu_slope(values):
    sigma = jax.nn.sigmoid(values)
    return sigma * (1.0 + values * (1.0 - sigma))


def position(cumulative_ref):
    rank = lax.axis_index("vox")
    return (rank, cumulative_ref[rank + 1] - cumulative_ref[rank], rank % 2 == 0)


def sides(first, second, even):
    return (jnp.where(even, second, first), jnp.where(even, first, second))


def row_mask(rows, live):
    return lax.broadcasted_iota(jnp.int32, (rows, 1), 0) < live


def place(ref, before, own, after, live):
    rows = own.shape[0]
    ref[:HALO, :] = before
    ref[HALO : HALO + rows, :] = own
    ref[HALO + rows :, :] = jnp.zeros((HALO, own.shape[1]), F32)
    ref[pl.ds(HALO + live, HALO), :] = after


def one_hot(index, rows, axis):
    shape = (rows, SPAN) if axis == 1 else (rows, index.shape[1])
    return (index == lax.broadcasted_iota(jnp.int32, shape, axis)).astype(F32).astype(BF16)


def gather_conv(ext, index_ref, kernel_ref, stash_ref, matrices, taken, halves, turned, sems, live):
    offsets, width = kernel_ref.shape[0], kernel_ref.shape[2]
    rows = index_ref.shape[1]
    blocks = rows // BLOCK
    fetch = pltpu.make_async_copy(kernel_ref, matrices, sems.at[blocks])
    fetch.start()
    high, low = split(ext[...])
    halves[:, :width] = high
    halves[:, width:] = low
    index = index_ref[...]
    index = jnp.where(index >= HALO + rows, index - rows + live, index)
    turned[:offsets, :] = index
    turned[offsets:, :] = jnp.full((turned.shape[0] - offsets, rows), -1, jnp.int32)
    stashes = []
    for b in range(blocks):
        window = halves[BLOCK * b : BLOCK * b + SPAN, :]
        columns = jnp.concatenate(
            [
                turned[:, BLOCK * b + HALO * h : BLOCK * b + HALO * (h + 1)].T
                for h in range(BLOCK // HALO)
            ],
            0,
        ) - (BLOCK * b)
        for k in range(offsets):
            hit = one_hot(columns[:, k : k + 1], BLOCK, 1)
            taken[k, BLOCK * b : BLOCK * (b + 1), :] = jnp.dot(
                hit, window, preferred_element_type=F32
            ).astype(BF16)
        part = (slice(None), pl.ds(BLOCK * b, BLOCK), slice(None))
        stashes.append(pltpu.make_async_copy(taken.at[part], stash_ref.at[part], sems.at[b]))
        stashes[b].start()
    fetch.wait()
    total = jnp.zeros((rows, 2 * width), F32)
    for k in range(offsets):
        both = jnp.concatenate(split(matrices[k]), 1)
        total = total + jnp.dot(
            taken[k], jnp.concatenate([both, both], 0), preferred_element_type=F32
        )
    for stash in stashes:
        stash.wait()
    return total[:, :width] + total[:, width:]


def scatter_conv(halves, target_ref, kernel_ref, blocks):
    offsets, width = kernel_ref.shape[0], kernel_ref.shape[2]
    total = jnp.zeros((len(blocks) * BLOCK, 2 * width), F32)
    for k in range(offsets):
        spread = []
        for b in blocks:
            index = target_ref[k : k + 1, BLOCK * b : BLOCK * b + SPAN] - BLOCK * b
            window = halves[BLOCK * b : BLOCK * b + SPAN, :]
            got = jnp.dot(one_hot(index, BLOCK, 0), window, preferred_element_type=F32)
            spread.append(jnp.concatenate(split(got[:, :width] + got[:, width:]), 1))
        tall = jnp.concatenate(split(kernel_ref[k]), 0)
        total = total + lax.dot_general(
            jnp.concatenate(spread, 0),
            jnp.concatenate([tall, tall], 1),
            (((1,), (1,)), ((), ())),
            preferred_element_type=F32,
        )
    return total[:, :width] + total[:, width:]


def kernel_grads(make_dy, stash_ref, taken, sems, store):
    offsets, width = taken.shape[0], taken.shape[2] // 2
    ends = [round(offsets * e) for e in CHUNKS]
    fetches = []
    for c, (start, end) in enumerate(zip(ends, ends[1:])):
        part = pl.ds(start, end - start)
        fetches.append(pltpu.make_async_copy(stash_ref.at[part], taken.at[part], sems.at[c]))
        fetches[c].start()
    turned = jnp.concatenate(split(make_dy().T), 0)
    for c, (start, end) in enumerate(zip(ends, ends[1:])):
        fetches[c].wait()
        for k in range(start, end):
            outer = jnp.dot(turned, taken[k], preferred_element_type=F32)
            outer = outer[:, :width] + outer[:, width:]
            store(k, (outer[:width] + outer[width:]).T)


class Ring:
    def __init__(self, count, tiles):
        bits = list(range(1, count.bit_length() - 1))
        self.orders = [bits, bits[1::-1] + bits[:1:-1], bits[2:] + bits[:2]]
        self.chips = count // 2
        self.tiles = tiles
        share = -(-tiles // self.chips)
        last = share * SHARE // 27
        first = (share - last + 1) // 2
        self.sizes = [first, share - last - first, last]
        self.starts = [self.chips * sum(self.sizes[:w]) for w in range(4)]
        self.padded = self.starts[3]

    def codes(self, rank):
        return [sum(((rank >> bit) & 1) << (len(order) - 1 - s) for s, bit in enumerate(order)) for order in self.orders]

    def store(self, ref, codes, first, value):
        for j in range(value.shape[0] // 8):
            part = sum(first + j >= start for start in self.starts[1:3])
            block, tile = divmod(first + j - self.starts[part], self.sizes[part])
            at = self.starts[part] + (block ^ codes[part]) * self.sizes[part] + tile
            ref[at] = value[8 * j : 8 * (j + 1), :]


def norm_stats(gathered_ref, cumulative_ref):
    count = gathered_ref.shape[0]
    total = cumulative_ref[count].astype(F32)
    mean = jnp.sum(gathered_ref[:, 0:1, :], 0) / total

    def step(d, spread):
        live = (cumulative_ref[d + 1] - cumulative_ref[d]).astype(F32)
        own = gathered_ref[d, 0:1, :] / live - mean
        return spread + gathered_ref[d, 1:2, :] + live * own * own

    spread = lax.fori_loop(0, count, step, jnp.zeros_like(mean))
    return (mean, lax.rsqrt(spread / total + EPS))


def share(stats_ref, first, second):
    both = jnp.concatenate([first, second], 0)
    stats_ref[...] = jnp.broadcast_to(both[None], stats_ref.shape)


def conv_stats(y, mask, live, stats_ref):
    first = jnp.sum(y, 0, keepdims=True)
    centred = jnp.where(mask, y - first / live.astype(F32), 0.0)
    share(stats_ref, first, jnp.sum(centred * centred, 0, keepdims=True))


def edges(first_ref, second_ref, ref, live, even):
    first_ref[:HALO, :] = ref[pl.ds(jnp.where(even, live - HALO, 0), HALO), :]
    second_ref[:HALO, :] = ref[pl.ds(jnp.where(even, 0, live - HALO), HALO), :]


def targets(target_ref, index_ref, before, after, live, rank, count, spread):
    rows = index_ref.shape[1]
    offsets = index_ref.shape[0]
    own = index_ref[...]
    own = jnp.where((own >= HALO) & (own < HALO + rows), own - HALO, -1)
    before = before.astype(jnp.int32) - (HALO + rows)
    before = jnp.where((before >= 0) & (rank > 0), before, -1)
    after = after.astype(jnp.int32)
    after = jnp.where(
        (after >= 0) & (after < HALO) & (rank < count - 1), after + live - HALO, -1
    )
    fill = jnp.full((target_ref.shape[0] - offsets, HALO), -1, jnp.int32)

    def turn(block):
        return jnp.concatenate([block, fill], 0).T

    spread[:HALO, :] = turn(before)
    for j in range(rows // HALO):
        spread[HALO * (j + 1) : HALO * (j + 2), :] = turn(own[:, HALO * j : HALO * (j + 1)])
    spread[HALO + rows :, :] = jnp.full((HALO, target_ref.shape[0]), -1, jnp.int32)
    spread[pl.ds(HALO + live, HALO), :] = turn(after)
    for j in range(target_ref.shape[1] // HALO):
        target_ref[:, HALO * j : HALO * (j + 1)] = spread[HALO * j : HALO * (j + 1), :].T


def pack_kernel(cumulative_ref, x_ref, first_ref, second_ref, head, near_tail, sems):
    _, live, even = position(cumulative_ref)
    tail = live - HALO
    start = pl.multiple_of(jnp.minimum(tail // 8 * 8, x_ref.shape[0] - near_tail.shape[0]), 8)
    fetches = [
        pltpu.make_async_copy(x_ref.at[pl.ds(0, HALO)], head, sems.at[0]),
        pltpu.make_async_copy(x_ref.at[pl.ds(start, near_tail.shape[0])], near_tail, sems.at[1]),
    ]
    for fetch in fetches:
        fetch.start()
    for fetch in fetches:
        fetch.wait()
    last = near_tail[pl.ds(tail - start, HALO), :]
    first_ref[...] = jnp.where(even, last, head[...])
    second_ref[...] = jnp.where(even, head[...], last)


def first_kernel(
    cumulative_ref, before_ref, after_ref, more1_ref, more2_ref, x_ref, neighbours_ref, kernel_ref,
    y_ref, swap1_ref, swap2_ref, stats_ref, stash_ref,
    index_ref, fetched, ext, *scratch,
):
    rows, width = x_ref.shape
    fetches = [
        pltpu.make_async_copy(x_ref, ext.at[pl.ds(HALO, rows)], fetched.at[0]),
        pltpu.make_async_copy(neighbours_ref, index_ref, fetched.at[1]),
    ]
    for fetch in fetches:
        fetch.start()
    _, live, even = position(cumulative_ref)
    before, after = sides(before_ref[...], after_ref[...], even)
    ext[:HALO, :] = before
    ext[HALO + rows :, :] = jnp.zeros((HALO, width), F32)
    for fetch in fetches:
        fetch.wait()
    ext[pl.ds(HALO + live, HALO), :] = after
    y = gather_conv(ext, index_ref, kernel_ref, stash_ref, *scratch, live)
    y_ref[...] = y
    conv_stats(y, row_mask(rows, live), live, stats_ref)
    edges(swap1_ref, swap2_ref, y_ref, live, even)
    swap1_ref[HALO:, :] = more1_ref[...]
    swap2_ref[HALO:, :] = more2_ref[...]


def second_kernel(
    cumulative_ref, y1_ref, swapped1_ref, swapped2_ref, gathered_ref, gain_ref, bias_ref,
    index_ref, kernel_ref,
    y_ref, swap1_ref, swap2_ref, stats_ref, stash_ref, target_ref, later_ref,
    spread, ext, *scratch,
):
    rank, live, even = position(cumulative_ref)
    count = gathered_ref.shape[0]
    mean, scale = norm_stats(gathered_ref, cumulative_ref)
    rows = y1_ref.shape[0]
    mask = row_mask(rows, live)

    def act(y):
        a = (y - mean) * scale * gain_ref[...] + bias_ref[...]
        return a * jax.nn.sigmoid(a)

    own = jnp.where(mask, act(y1_ref[...]), 0.0)
    before, after = sides(swapped1_ref[:HALO, :], swapped2_ref[:HALO, :], even)
    before = jnp.where(rank > 0, act(before), 0.0)
    after = jnp.where(rank < count - 1, act(after), 0.0)
    place(ext, before, own, after, live)
    before, after = sides(swapped1_ref[2 * HALO :, :], swapped2_ref[2 * HALO :, :], even)
    targets(target_ref, index_ref, before, after, live, rank, count, spread)
    later_ref[...] = target_ref[...]
    y = gather_conv(ext, index_ref, kernel_ref, stash_ref, *scratch, live)
    y_ref[...] = y
    conv_stats(y, mask, live, stats_ref)
    edges(swap1_ref, swap2_ref, y_ref, live, even)


def middle_kernel(
    cumulative_ref, y_ref, y_swap1_ref, y_swap2_ref, gathered_ref, gain_ref, bias_ref,
    x_ref, x_swap1_ref, x_swap2_ref, swapped1_ref, swapped2_ref, cotangent_ref,
    out_ref, dpre_ref, dz_ref, unit_ref, stats_ref,
):
    _, live, even = position(cumulative_ref)
    mean, scale = norm_stats(gathered_ref, cumulative_ref)
    mask = row_mask(x_ref.shape[0], live)

    def part(y, x, cotangent):
        unit = (y - mean) * scale
        pre = unit * gain_ref[...] + bias_ref[...] + x
        return (unit, pre, cotangent * silu_slope(pre))

    unit, pre, dz = part(y_ref[...], x_ref[...], cotangent_ref[...])
    dz = jnp.where(mask, dz, 0.0)
    dpre_ref[...] = dz
    out_ref[...] = jnp.where(mask, pre * jax.nn.sigmoid(pre), 0.0)
    share(
        stats_ref, jnp.sum(dz, 0, keepdims=True), jnp.sum(dz * unit, 0, keepdims=True)
    )
    y_before, y_after = sides(y_swap1_ref[...], y_swap2_ref[...], even)
    x_before, x_after = sides(x_swap1_ref[...], x_swap2_ref[...], even)
    more = slice(HALO, 2 * HALO)
    before, after = sides(swapped1_ref[more, :], swapped2_ref[more, :], even)
    unit_b, _, dz_b = part(y_before, x_before, before)
    unit_a, _, dz_a = part(y_after, x_after, after)
    place(dz_ref, dz_b, dz, dz_a, live)
    place(unit_ref, unit_b, unit, unit_a, live)


def norm_back(dz, unit, scale, gain, gathered_ref, total):
    dbias = jnp.sum(gathered_ref[:, 0:1, :], 0)
    dgain = jnp.sum(gathered_ref[:, 1:2, :], 0)
    slope = scale * gain
    return (slope * dz - slope * dbias / total - unit * (slope * dgain / total), dgain, dbias)


def back_two_kernel(
    cumulative_ref, dz_ref, unit_ref, stats2_ref, back_ref, gain2_ref, target_ref,
    y1_ref, stats1_ref, gain1_ref, bias1_ref, kernel_ref,
    dy_ref, dz1_ref, swap1_ref, swap2_ref, stats_ref, dgain_ref, dbias_ref,
    halves,
):
    _, live, even = position(cumulative_ref)
    count = stats1_ref.shape[0]
    total = cumulative_ref[count].astype(F32)
    rows, width = y1_ref.shape
    _, scale2 = norm_stats(stats2_ref, cumulative_ref)
    dy, dgain, dbias = norm_back(
        dz_ref[...], unit_ref[...], scale2, gain2_ref[...], back_ref, total
    )
    dgain_ref[...] = dgain
    dbias_ref[...] = dbias
    dy_ref[...] = dy[HALO : HALO + rows]
    high, low = split(dy)
    halves[:, :width] = high
    halves[:, width:] = low
    dhidden = scatter_conv(halves, target_ref, kernel_ref, range(rows // BLOCK))
    mean1, scale1 = norm_stats(stats1_ref, cumulative_ref)
    unit1 = (y1_ref[...] - mean1) * scale1
    slope = silu_slope(unit1 * gain1_ref[...] + bias1_ref[...])
    dz1 = jnp.where(row_mask(rows, live), dhidden * slope, 0.0)
    dz1_ref[...] = dz1
    share(stats_ref, jnp.sum(dz1, 0, keepdims=True), jnp.sum(dz1 * unit1, 0, keepdims=True))
    edges(swap1_ref, swap2_ref, dz1_ref, live, even)


def grad_two_kernel(ring, dy_ref, stash_ref, grad_ref, taken, sems):
    codes = ring.codes(lax.axis_index("vox"))

    def store(k, value):
        ring.store(grad_ref, codes, k * (value.shape[0] // 8), value)

    kernel_grads(lambda: dy_ref[...], stash_ref, taken, sems, store)


def grad_one_kernel(
    ring,
    cumulative_ref, dz_ref, swap1_ref, swap2_ref, y_ref, y_swap1_ref, y_swap2_ref,
    stats_ref, back_ref, gain_ref, two_ref, stash_ref,
    keep_ref, give_ref, halves_ref, dgain_ref, dbias_ref,
    ext, grad, taken, sems,
):
    rank, live, even = position(cumulative_ref)
    total = cumulative_ref[stats_ref.shape[0]].astype(F32)
    width = y_ref.shape[1]
    codes = ring.codes(rank)

    def make_dy():
        mean, scale = norm_stats(stats_ref, cumulative_ref)

        def part(dz, y):
            return norm_back(dz, (y - mean) * scale, scale, gain_ref[...], back_ref, total)

        dz_before, dz_after = sides(swap1_ref[...], swap2_ref[...], even)
        y_before, y_after = sides(y_swap1_ref[:HALO, :], y_swap2_ref[:HALO, :], even)
        dy, dgain, dbias = part(dz_ref[...], y_ref[...])
        dgain_ref[...] = dgain
        dbias_ref[...] = dbias
        place(ext, part(dz_before, y_before)[0], dy, part(dz_after, y_after)[0], live)
        high, low = split(ext[...])
        halves_ref[:, :width] = high
        halves_ref[:, width:] = low
        return dy

    def store(k, value):
        ring.store(grad, codes, k * (value.shape[0] // 8), value)

    kernel_grads(make_dy, stash_ref, taken, sems, store)
    keep_ref[...] = jnp.where(even, two_ref[...], grad[...])
    give_ref[...] = jnp.where(even, grad[...], two_ref[...])


def back_one_kernel(
    block, halves_ref, target_ref, dpre_ref, kernel_ref, *refs
):
    dx_ref, zero_ref, result, sem = refs[-4:]
    rows = BLOCK * block
    dx = scatter_conv(halves_ref, target_ref, kernel_ref, (block,))
    result[...] = dx + dpre_ref[rows : rows + BLOCK, :]
    store = pltpu.make_async_copy(result, dx_ref.at[pl.ds(rows, BLOCK)], sem)
    store.start()
    zero_ref[...] = jnp.zeros_like(zero_ref)
    store.wait()


def finish_kernel(ring, *refs):
    count = len(ring.orders)
    low, high, low_other, high_other = (refs[i * count : (i + 1) * count] for i in range(4))
    one_ref, two_ref, sems = refs[4 * count :]
    rank = lax.axis_index("vox")
    codes = ring.codes(rank)
    half = ring.chips // 2

    def spread(pieces, ref, sem):
        for part, halves in enumerate(zip(*pieces)):
            for block in range(ring.chips):
                size = ring.sizes[part]
                at = ring.starts[part] + (block ^ codes[part]) * size
                pltpu.make_async_copy(
                    halves[block // half].at[pl.ds(block % half * size, size)],
                    ref.at[pl.ds(at, size)],
                    sem,
                ).start()

    def finish(own_ref, other_ref):
        spread((low, high), own_ref, sems.at[0])
        spread((low_other, high_other), other_ref, sems.at[1])
        for i, ref in enumerate((own_ref, other_ref)):
            pltpu.make_async_copy(ref, ref, sems.at[i]).wait()

    @pl.when(rank % 2 == 0)
    def _():
        finish(two_ref, one_ref)

    @pl.when(rank % 2 == 1)
    def _():
        finish(one_ref, two_ref)


def run(body, cumulative, arrays, outs, scratch, flops=0, limit=28, aliases=None):
    plain = pl.BlockSpec(memory_space=pltpu.VMEM)
    there = pl.BlockSpec(memory_space=pltpu.MemorySpace.HBM)
    shapes, out_specs = [], []
    for out in outs:
        if out[0] == "near":
            shapes.append(pltpu.VMEM(*out[1:]))
            out_specs.append(plain)
        elif out[0] == "here":
            shapes.append(jax.ShapeDtypeStruct(*out[1:]))
            out_specs.append(plain)
        elif out[0] == "far":
            shapes.append(pltpu.MemorySpace.HBM(*out[1:]))
            out_specs.append(there)
        else:
            shapes.append(jax.ShapeDtypeStruct(out, F32))
            out_specs.append(plain)
    any_space = pl.BlockSpec(memory_space=pl.ANY)
    operands, specs = [], []
    if cumulative is not None:
        operands.append(pltpu.with_memory_space_constraint(cumulative, pltpu.MemorySpace.HBM))
        specs.append(pl.BlockSpec(memory_space=pltpu.SMEM))
    for array in arrays:
        how, array = array if isinstance(array, tuple) else ("near", array)
        specs.append({"near": plain, "here": plain, "far": there, "any": any_space}[how])
        if how in ("near", "far"):
            space = pltpu.VMEM if how == "near" else pltpu.MemorySpace.HBM
            array = pltpu.with_memory_space_constraint(array, space)
        operands.append(array)
    return pl.pallas_call(
        body,
        in_specs=specs,
        out_specs=out_specs,
        out_shape=shapes,
        scratch_shapes=scratch,
        input_output_aliases=aliases or {},
        cost_estimate=pl.CostEstimate(flops=flops, bytes_accessed=2**20, transcendentals=0),
        compiler_params=pltpu.CompilerParams(vmem_limit_bytes=limit * 2**20),
    )(*operands)


def sum_chips(ring, pairs, swap_chips, swap_cores, beside, zero):
    stages = len(ring.orders[0])
    for stage in range(stages):
        wider = []
        for (a, b), order in zip(pairs, ring.orders):
            half = a.shape[0] // 2
            sent = a[half:] + b[half:]
            if zero is not None:
                sent = sent + zero
            wider.append((a[:half] + b[:half], swap_chips(sent, order[stage])))
        pairs = wider
        zero = beside(sent) if stage in BESIDE[0] else None
    pieces = [a + b for a, b in pairs]
    for stage in reversed(range(1, stages)):
        got = [swap_chips(piece, order[stage]) for piece, order in zip(pieces, ring.orders)]
        zero = beside(pieces[-1]) if stage in BESIDE[1] else None
        pieces = [jnp.concatenate(both, 0) for both in zip(pieces, got)]
        if zero is not None:
            pieces = [piece + zero for piece in pieces]
    highs = [swap_chips(piece, order[0]) for piece, order in zip(pieces, ring.orders)]
    zero = beside(pieces[-1])
    highs[LATE] = highs[LATE] + zero
    return (*pieces, *highs, *map(swap_cores, pieces), *map(swap_cores, highs))


def per_device(
    features,
    kernel_one,
    gain_one,
    bias_one,
    kernel_two,
    gain_two,
    bias_two,
    cotangent,
    cumulative,
    neighbours,
):
    rank = lax.axis_index("vox")
    count = cumulative.shape[0] - 1
    ends = lax.dynamic_slice(cumulative, (rank,), (2,), allow_negative_indices=False)
    tail = ends[1] - ends[0] - HALO
    rows, width = features.shape
    offsets = neighbours.shape[0]
    even = rank % 2 == 0
    gain_one, bias_one = gain_one[None], bias_one[None]
    gain_two, bias_two = gain_two[None], bias_two[None]

    def swap(first, second):
        within = [(i, i ^ 1) for i in range(count)]
        across = [(i, i + 1) for i in range(1, count - 1, 2)]
        across = across + [(j, i) for i, j in across]
        return (lax.ppermute(first, "vox", within), lax.ppermute(second, "vox", across))

    def spread(stats):
        return lax.all_to_all(stats, "vox", 0, 0)

    def more(start):
        def part(array, shape, where):
            return lax.dynamic_slice(array, where, shape, allow_negative_indices=False)

        zero = jnp.zeros_like(start)
        return jnp.concatenate(
            [
                part(cotangent, (HALO, width), (start, zero)),
                part(neighbours, (offsets, HALO), (zero, start)).astype(F32),
            ],
            0,
        )

    ext_shape = (rows + 2 * HALO, width)
    stats_shape = (count, 2, width)
    edge = (HALO, width)
    wide_edge = (2 * HALO + offsets, width)
    vector = (1, width)
    turned_rows = -(-offsets // 8) * 8
    taken = (offsets, rows, 2 * width)
    halves = (ext_shape[0], 2 * width)
    conv_scratch = [
        pltpu.VMEM(ext_shape, F32),
        pltpu.VMEM((offsets, width, width), F32),
        pltpu.VMEM(taken, BF16),
        pltpu.VMEM(halves, BF16),
        pltpu.VMEM((turned_rows, rows), jnp.int32),
        pltpu.SemaphoreType.DMA((rows // BLOCK + 1,)),
    ]
    grad_scratch = [pltpu.VMEM(taken, BF16), pltpu.SemaphoreType.DMA((len(CHUNKS) - 1,))]
    x_edges = swap(
        *run(
            pack_kernel,
            cumulative,
            (("far", features),),
            (edge, edge),
            [pltpu.VMEM(edge, F32), pltpu.VMEM((HALO + 8, width), F32), pltpu.SemaphoreType.DMA((2,))],
        )
    )
    mores = (more(jnp.where(even, tail, 0)), more(jnp.where(even, 0, tail)))
    ring = Ring(count, offsets * width // 8)
    grad = (ring.padded, 8, width)
    work = 2 * offsets * rows * width * width * 4

    def move(piece, pairs):
        return lax.ppermute(piece, "vox", pairs)

    def near(shape, kind=F32):
        return ("near", shape, kind)

    y1, swap1, swap2, stats, stash1 = run(
        first_kernel,
        cumulative,
        (*x_edges, *mores, ("far", features), ("far", neighbours), ("far", kernel_one)),
        (near((rows, width)), wide_edge, wide_edge, stats_shape, ("far", taken, BF16)),
        [
            pltpu.VMEM(neighbours.shape, jnp.int32),
            pltpu.SemaphoreType.DMA((2,)),
            *conv_scratch,
        ],
        flops=3 * work,
    )
    y1_edges = swap(swap1, swap2)
    stats1 = spread(stats)
    y2, swap1, swap2, stats, stash2, target, later_target = run(
        second_kernel,
        cumulative,
        (y1, *y1_edges, stats1, gain_one, bias_one, neighbours, ("far", kernel_two)),
        (
            near((rows, width)), edge, edge, stats_shape, ("far", taken, BF16),
            near((turned_rows, ext_shape[0]), jnp.int32),
            ("here", (turned_rows, ext_shape[0]), jnp.int32),
        ),
        [pltpu.VMEM((ext_shape[0], turned_rows), jnp.int32), *conv_scratch],
        flops=3 * work,
    )
    y2_edges = swap(swap1, swap2)
    stats2 = spread(stats)
    output, dpre, dz2, unit2, stats = run(
        middle_kernel,
        cumulative,
        (
            y2, *y2_edges, stats2, gain_two, bias_two, features, *x_edges, *y1_edges, cotangent,
        ),
        ((rows, width), (rows, width), near(ext_shape), near(ext_shape), stats_shape),
        [],
    )
    back2 = spread(stats)
    dy2, dz1, swap1, swap2, stats, dgain_two, dbias_two = run(
        back_two_kernel,
        cumulative,
        (
            dz2, unit2, stats2, back2, gain_two, target, y1, stats1, gain_one, bias_one,
            kernel_two,
        ),
        (near((rows, width)), near((rows, width)), edge, edge, stats_shape, vector, vector),
        [pltpu.VMEM(halves, BF16)],
        flops=3 * work,
    )
    dz_edges = swap(swap1, swap2)
    back1 = spread(stats)
    (two,) = run(
        functools.partial(grad_two_kernel, ring),
        None,
        (dy2, ("far", stash2)),
        (near(grad),),
        grad_scratch,
        flops=work,
    )
    keep, give, halves_one, dgain_one, dbias_one = run(
        functools.partial(grad_one_kernel, ring),
        cumulative,
        (
            dz1, *dz_edges, y1, *y1_edges, stats1, back1, gain_one, two, ("far", stash1),
        ),
        (grad, grad, near(halves, BF16), vector, vector),
        [pltpu.VMEM(ext_shape, F32), pltpu.VMEM(grad, F32), *grad_scratch],
        flops=work,
    )
    theirs = move(give, [(i, i ^ 1) for i in range(count)])
    dx = None
    blocks = list(range(rows // BLOCK))

    def beside(sent):
        nonlocal dx
        block = blocks.pop(0)
        arrays = (halves_one, later_target, dpre, kernel_one, ("any", sent))
        dx, zero = run(
            functools.partial(back_one_kernel, block),
            None,
            arrays if dx is None else (*arrays, ("far", dx)),
            (("far", (rows, width), F32), (8, width)),
            [pltpu.VMEM((BLOCK, width), F32), pltpu.SemaphoreType.DMA],
            flops=3 * work // (rows // BLOCK),
            aliases=None if dx is None else {len(arrays): 0},
        )
        return zero

    def part(array, w):
        return array[ring.starts[w] : ring.starts[w + 1]]

    sums = sum_chips(
        ring,
        [(part(keep, w), part(theirs, w)) for w in range(len(ring.orders))],
        lambda piece, bit: move(piece, [(i, i ^ (1 << bit)) for i in range(count)]),
        lambda piece: move(piece, [(i, i ^ 1) for i in range(count)]),
        beside,
        beside(give),
    )
    grads = run(
        functools.partial(finish_kernel, ring),
        None,
        [("any", piece) for piece in sums],
        (("far", grad, F32), ("far", grad, F32)),
        [pltpu.SemaphoreType.DMA((2,))],
    )
    dkernel_one, dkernel_two = (
        array[: ring.tiles].reshape(offsets, width, width) for array in grads
    )
    return (
        output,
        dx,
        dkernel_one,
        dkernel_two,
        dgain_one[0],
        dbias_one[0],
        dgain_two[0],
        dbias_two[0],
    )


def solution(mesh):
    return jax.shard_map(
        per_device,
        mesh=mesh,
        in_specs=(
            P("vox", None),
            P(),
            P(),
            P(),
            P(),
            P(),
            P(),
            P("vox", None),
            P(),
            P(None, "vox"),
        ),
        out_specs=(P("vox", None), P("vox", None), P(), P(), P(), P(), P(), P()),
        check_vma=False,
    )
```

```python
import functools

import jax
import jax.numpy as jnp
from jax import lax
from jax.experimental import pallas as pl
from jax.experimental.pallas import tpu as pltpu
from jax.sharding import PartitionSpec as P

HALO = 128
BLOCK = 256
SPAN = BLOCK + 2 * HALO
EPS = 1e-05
SHARE = 9
BESIDE = ((0,), (1,))
LATE = 2
CHUNKS = (0.0, 0.4, 0.75, 1.0)
F32 = jnp.float32
BF16 = jnp.bfloat16


def split(values):
    high = values.astype(BF16)
    low = (values - high.astype(F32)).astype(BF16)
    return (high, low)


def silu_slope(values):
    sigma = jax.nn.sigmoid(values)
    return sigma * (1.0 + values * (1.0 - sigma))


def position(cumulative_ref):
    rank = lax.axis_index("vox")
    return (rank, cumulative_ref[rank + 1] - cumulative_ref[rank], rank % 2 == 0)


def sides(first, second, even):
    return (jnp.where(even, second, first), jnp.where(even, first, second))


def row_mask(rows, live):
    return lax.broadcasted_iota(jnp.int32, (rows, 1), 0) < live


def place(ref, before, own, after, live):
    rows = own.shape[0]
    ref[:HALO, :] = before
    ref[HALO : HALO + rows, :] = own
    ref[HALO + rows :, :] = jnp.zeros((HALO, own.shape[1]), F32)
    ref[pl.ds(HALO + live, HALO), :] = after


def one_hot(index, rows, axis):
    shape = (SPAN, rows) if axis == 0 else (rows, index.shape[1])
    return (index == lax.broadcasted_iota(jnp.int32, shape, 0)).astype(F32).astype(BF16)


def gather_conv(ext, index_ref, kernel_ref, stash_ref, matrices, taken, turned, halves, sems, live):
    offsets, width = kernel_ref.shape[0], kernel_ref.shape[2]
    rows = index_ref.shape[1]
    chunks = sems.shape[0] - 1
    fetch = pltpu.make_async_copy(kernel_ref, matrices, sems.at[chunks])
    fetch.start()
    for j in range(ext.shape[0] // HALO):
        at = slice(HALO * j, HALO * (j + 1))
        turned[:, at] = ext[at, :].T
        halves[:width, at], halves[width:, at] = split(turned[:, at])
    index = index_ref[...]
    index = jnp.where(index >= HALO + rows, index - rows + live, index)

    def by_product(k, start):
        hit = one_hot(index[k : k + 1, start : start + BLOCK] - start, BLOCK, 0)
        window = halves[:, start : start + SPAN]
        got = jnp.dot(window, hit, preferred_element_type=F32)
        taken[k, :, start : start + BLOCK] = got.astype(BF16)

    def by_lanes(k, start):
        place = index[k : k + 1, start : start + HALO] - start
        piece = jnp.broadcast_to(lax.shift_right_arithmetic(place, 7), (width, HALO))
        lane = jnp.broadcast_to(lax.bitwise_and(place, HALO - 1), (width, HALO))
        total = jnp.zeros((width, HALO), F32)
        for p in range(2, -1, -1):
            block = turned[:, start + HALO * p : start + HALO * (p + 1)]
            got = jnp.take_along_axis(block, lane, axis=1, mode="promise_in_bounds")
            total = jnp.where(piece == p, got, total)
        at = slice(start, start + HALO)
        taken[k, :width, at], taken[k, width:, at] = split(total)

    ends = [offsets * c // chunks for c in range(chunks + 1)]
    stashes = []
    for c in range(chunks):
        for k in range(ends[c], ends[c + 1]):
            for start in range(0, rows // 2, BLOCK):
                by_product(k, start)
            for start in range(rows // 2, rows, HALO):
                by_lanes(k, start)
        part = pl.ds(ends[c], ends[c + 1] - ends[c])
        stashes.append(pltpu.make_async_copy(taken.at[part], stash_ref.at[part], sems.at[c]))
        stashes[c].start()
    fetch.wait()
    total = jnp.zeros((2 * width, rows), F32)
    for k in range(offsets):
        both = jnp.concatenate(split(matrices[k].T), 0)
        total = total + jnp.dot(
            jnp.concatenate([both, both], 1), taken[k], preferred_element_type=F32
        )
    total = total[:width] + total[width:]
    for stash in stashes:
        stash.wait()
    return jnp.concatenate(
        [total[:, HALO * j : HALO * (j + 1)].T for j in range(rows // HALO)], 0
    )


def scatter_conv(halves, target_ref, kernel_ref, blocks):
    offsets, width = kernel_ref.shape[0], kernel_ref.shape[2]
    total = jnp.zeros((len(blocks) * BLOCK, 2 * width), F32)
    for k in range(offsets):
        spread = []
        for b in blocks:
            index = target_ref[k : k + 1, BLOCK * b : BLOCK * b + SPAN] - BLOCK * b
            window = halves[BLOCK * b : BLOCK * b + SPAN, :]
            got = jnp.dot(one_hot(index, BLOCK, 1), window, preferred_element_type=F32)
            spread.append(jnp.concatenate(split(got[:, :width] + got[:, width:]), 1))
        tall = jnp.concatenate(split(kernel_ref[k]), 0)
        total = total + lax.dot_general(
            jnp.concatenate(spread, 0),
            jnp.concatenate([tall, tall], 1),
            (((1,), (1,)), ((), ())),
            preferred_element_type=F32,
        )
    return total[:, :width] + total[:, width:]


def kernel_grads(make_dy, stash_ref, taken, sems, store):
    offsets, width = taken.shape[0], taken.shape[1] // 2
    ends = [round(offsets * e) for e in CHUNKS]
    fetches = []
    for c, (start, end) in enumerate(zip(ends, ends[1:])):
        part = pl.ds(start, end - start)
        fetches.append(pltpu.make_async_copy(stash_ref.at[part], taken.at[part], sems.at[c]))
        fetches[c].start()
    wide = jnp.concatenate(split(make_dy()), 1)
    for c, (start, end) in enumerate(zip(ends, ends[1:])):
        fetches[c].wait()
        for k in range(start, end):
            outer = jnp.dot(taken[k], wide, preferred_element_type=F32)
            outer = outer[:, :width] + outer[:, width:]
            store(k, outer[:width] + outer[width:])


class Ring:
    def __init__(self, count, tiles):
        bits = list(range(1, count.bit_length() - 1))
        x, y, z = bits[:3]
        self.orders = [[*order, *bits[3:]] for order in ((x, z, y), (y, x, z), (z, y, x))]
        self.chips = count // 2
        self.tiles = tiles
        share = -(-tiles // self.chips)
        last = share * SHARE // 27
        first = (share - last + 1) // 2
        self.sizes = [first, share - last - first, last]
        self.starts = [self.chips * sum(self.sizes[:w]) for w in range(4)]
        self.padded = self.starts[3]

    def codes(self, rank):
        return [sum(((rank >> bit) & 1) << (len(order) - 1 - s) for s, bit in enumerate(order)) for order in self.orders]

    def store(self, ref, codes, first, value):
        for j in range(value.shape[0] // 8):
            part = sum(first + j >= start for start in self.starts[1:3])
            block, tile = divmod(first + j - self.starts[part], self.sizes[part])
            at = self.starts[part] + (block ^ codes[part]) * self.sizes[part] + tile
            ref[at] = value[8 * j : 8 * (j + 1), :]


def norm_stats(gathered_ref, cumulative_ref):
    count = gathered_ref.shape[0]
    total = cumulative_ref[count].astype(F32)
    mean = jnp.sum(gathered_ref[:, 0:1, :], 0) / total

    def step(d, spread):
        live = (cumulative_ref[d + 1] - cumulative_ref[d]).astype(F32)
        own = gathered_ref[d, 0:1, :] / live - mean
        return spread + gathered_ref[d, 1:2, :] + live * own * own

    spread = lax.fori_loop(0, count, step, jnp.zeros_like(mean))
    return (mean, lax.rsqrt(spread / total + EPS))


def share(stats_ref, first, second):
    both = jnp.concatenate([first, second], 0)
    stats_ref[...] = jnp.broadcast_to(both[None], stats_ref.shape)


def conv_stats(y, mask, live, stats_ref):
    first = jnp.sum(y, 0, keepdims=True)
    centred = jnp.where(mask, y - first / live.astype(F32), 0.0)
    share(stats_ref, first, jnp.sum(centred * centred, 0, keepdims=True))


def edges(first_ref, second_ref, ref, live, even):
    first_ref[:HALO, :] = ref[pl.ds(jnp.where(even, live - HALO, 0), HALO), :]
    second_ref[:HALO, :] = ref[pl.ds(jnp.where(even, 0, live - HALO), HALO), :]


def targets(target_ref, index_ref, before, after, live, rank, count, spread):
    rows = index_ref.shape[1]
    offsets = index_ref.shape[0]
    own = index_ref[...]
    own = jnp.where((own >= HALO) & (own < HALO + rows), own - HALO, -1)
    before = before.astype(jnp.int32) - (HALO + rows)
    before = jnp.where((before >= 0) & (rank > 0), before, -1)
    after = after.astype(jnp.int32)
    after = jnp.where(
        (after >= 0) & (after < HALO) & (rank < count - 1), after + live - HALO, -1
    )
    fill = jnp.full((target_ref.shape[0] - offsets, HALO), -1, jnp.int32)

    def turn(block):
        return jnp.concatenate([block, fill], 0).T

    spread[:HALO, :] = turn(before)
    for j in range(rows // HALO):
        spread[HALO * (j + 1) : HALO * (j + 2), :] = turn(own[:, HALO * j : HALO * (j + 1)])
    spread[HALO + rows :, :] = jnp.full((HALO, target_ref.shape[0]), -1, jnp.int32)
    spread[pl.ds(HALO + live, HALO), :] = turn(after)
    for j in range(target_ref.shape[1] // HALO):
        target_ref[:, HALO * j : HALO * (j + 1)] = spread[HALO * j : HALO * (j + 1), :].T


def pack_kernel(cumulative_ref, x_ref, first_ref, second_ref, head, near_tail, sems):
    _, live, even = position(cumulative_ref)
    tail = live - HALO
    start = pl.multiple_of(jnp.minimum(tail // 8 * 8, x_ref.shape[0] - near_tail.shape[0]), 8)
    fetches = [
        pltpu.make_async_copy(x_ref.at[pl.ds(0, HALO)], head, sems.at[0]),
        pltpu.make_async_copy(x_ref.at[pl.ds(start, near_tail.shape[0])], near_tail, sems.at[1]),
    ]
    for fetch in fetches:
        fetch.start()
    for fetch in fetches:
        fetch.wait()
    last = near_tail[pl.ds(tail - start, HALO), :]
    first_ref[...] = jnp.where(even, last, head[...])
    second_ref[...] = jnp.where(even, head[...], last)


def first_kernel(
    cumulative_ref, before_ref, after_ref, more1_ref, more2_ref, x_ref, neighbours_ref, kernel_ref,
    y_ref, swap1_ref, swap2_ref, stats_ref, stash_ref,
    index_ref, fetched, ext, *scratch,
):
    rows, width = x_ref.shape
    fetches = [
        pltpu.make_async_copy(x_ref, ext.at[pl.ds(HALO, rows)], fetched.at[0]),
        pltpu.make_async_copy(neighbours_ref, index_ref, fetched.at[1]),
    ]
    for fetch in fetches:
        fetch.start()
    _, live, even = position(cumulative_ref)
    before, after = sides(before_ref[...], after_ref[...], even)
    ext[:HALO, :] = before
    ext[HALO + rows :, :] = jnp.zeros((HALO, width), F32)
    for fetch in fetches:
        fetch.wait()
    ext[pl.ds(HALO + live, HALO), :] = after
    y = gather_conv(ext, index_ref, kernel_ref, stash_ref, *scratch, live)
    y_ref[...] = y
    conv_stats(y, row_mask(rows, live), live, stats_ref)
    edges(swap1_ref, swap2_ref, y_ref, live, even)
    swap1_ref[HALO:, :] = more1_ref[...]
    swap2_ref[HALO:, :] = more2_ref[...]


def second_kernel(
    cumulative_ref, y1_ref, swapped1_ref, swapped2_ref, gathered_ref, gain_ref, bias_ref,
    index_ref, kernel_ref,
    y_ref, swap1_ref, swap2_ref, stats_ref, stash_ref, target_ref, later_ref,
    spread, sent, ext, *scratch,
):
    rank, live, even = position(cumulative_ref)
    count = gathered_ref.shape[0]
    mean, scale = norm_stats(gathered_ref, cumulative_ref)
    rows = y1_ref.shape[0]
    mask = row_mask(rows, live)

    def act(y):
        a = (y - mean) * scale * gain_ref[...] + bias_ref[...]
        return a * jax.nn.sigmoid(a)

    own = jnp.where(mask, act(y1_ref[...]), 0.0)
    before, after = sides(swapped1_ref[:HALO, :], swapped2_ref[:HALO, :], even)
    before = jnp.where(rank > 0, act(before), 0.0)
    after = jnp.where(rank < count - 1, act(after), 0.0)
    place(ext, before, own, after, live)
    before, after = sides(swapped1_ref[2 * HALO :, :], swapped2_ref[2 * HALO :, :], even)
    targets(target_ref, index_ref, before, after, live, rank, count, spread)
    later = pltpu.make_async_copy(target_ref, later_ref, sent)
    later.start()
    y = gather_conv(ext, index_ref, kernel_ref, stash_ref, *scratch, live)
    y_ref[...] = y
    conv_stats(y, mask, live, stats_ref)
    edges(swap1_ref, swap2_ref, y_ref, live, even)
    later.wait()


def middle_kernel(
    cumulative_ref, y_ref, y_swap1_ref, y_swap2_ref, gathered_ref, gain_ref, bias_ref,
    x_ref, x_swap1_ref, x_swap2_ref, swapped1_ref, swapped2_ref, cotangent_ref,
    out_ref, dz_ref, unit_ref, stats_ref,
):
    _, live, even = position(cumulative_ref)
    mean, scale = norm_stats(gathered_ref, cumulative_ref)
    mask = row_mask(x_ref.shape[0], live)

    def part(y, x, cotangent):
        unit = (y - mean) * scale
        pre = unit * gain_ref[...] + bias_ref[...] + x
        return (unit, pre, cotangent * silu_slope(pre))

    unit, pre, dz = part(y_ref[...], x_ref[...], cotangent_ref[...])
    dz = jnp.where(mask, dz, 0.0)
    out_ref[...] = jnp.where(mask, pre * jax.nn.sigmoid(pre), 0.0)
    share(
        stats_ref, jnp.sum(dz, 0, keepdims=True), jnp.sum(dz * unit, 0, keepdims=True)
    )
    y_before, y_after = sides(y_swap1_ref[...], y_swap2_ref[...], even)
    x_before, x_after = sides(x_swap1_ref[...], x_swap2_ref[...], even)
    more = slice(HALO, 2 * HALO)
    before, after = sides(swapped1_ref[more, :], swapped2_ref[more, :], even)
    unit_b, _, dz_b = part(y_before, x_before, before)
    unit_a, _, dz_a = part(y_after, x_after, after)
    place(dz_ref, dz_b, dz, dz_a, live)
    place(unit_ref, unit_b, unit, unit_a, live)


def norm_back(dz, unit, scale, gain, gathered_ref, total):
    dbias = jnp.sum(gathered_ref[:, 0:1, :], 0)
    dgain = jnp.sum(gathered_ref[:, 1:2, :], 0)
    slope = scale * gain
    return (slope * dz - slope * dbias / total - unit * (slope * dgain / total), dgain, dbias)


def back_two_kernel(
    cumulative_ref, dz_ref, unit_ref, stats2_ref, back_ref, gain2_ref, target_ref,
    y1_ref, stats1_ref, gain1_ref, bias1_ref, kernel_ref,
    dy_ref, dpre_ref, dz1_ref, swap1_ref, swap2_ref, stats_ref, dgain_ref, dbias_ref,
    halves, own, sent,
):
    _, live, even = position(cumulative_ref)
    count = stats1_ref.shape[0]
    total = cumulative_ref[count].astype(F32)
    rows, width = y1_ref.shape
    _, scale2 = norm_stats(stats2_ref, cumulative_ref)
    dy, dgain, dbias = norm_back(
        dz_ref[...], unit_ref[...], scale2, gain2_ref[...], back_ref, total
    )
    dgain_ref[...] = dgain
    dbias_ref[...] = dbias
    mask = row_mask(rows, live)
    own[0] = dy[HALO : HALO + rows]
    own[1] = jnp.where(mask, dz_ref[HALO : HALO + rows, :], 0.0)
    later = [
        pltpu.make_async_copy(own.at[i], ref, sent.at[i]) for i, ref in enumerate((dy_ref, dpre_ref))
    ]
    for copy in later:
        copy.start()
    high, low = split(dy)
    halves[:, :width] = high
    halves[:, width:] = low
    dhidden = scatter_conv(halves, target_ref, kernel_ref, range(rows // BLOCK))
    mean1, scale1 = norm_stats(stats1_ref, cumulative_ref)
    unit1 = (y1_ref[...] - mean1) * scale1
    slope = silu_slope(unit1 * gain1_ref[...] + bias1_ref[...])
    dz1 = jnp.where(mask, dhidden * slope, 0.0)
    dz1_ref[...] = dz1
    share(stats_ref, jnp.sum(dz1, 0, keepdims=True), jnp.sum(dz1 * unit1, 0, keepdims=True))
    edges(swap1_ref, swap2_ref, dz1_ref, live, even)
    for copy in later:
        copy.wait()


def grad_two_kernel(ring, dy_ref, stash_ref, grad_ref, own_dy, sent, taken, sems):
    fetch = pltpu.make_async_copy(dy_ref, own_dy, sent)
    fetch.start()
    codes = ring.codes(lax.axis_index("vox"))

    def store(k, value):
        ring.store(grad_ref, codes, k * (value.shape[0] // 8), value)

    def make_dy():
        fetch.wait()
        return own_dy[...]

    kernel_grads(make_dy, stash_ref, taken, sems, store)


def grad_one_kernel(
    ring,
    cumulative_ref, dz_ref, swap1_ref, swap2_ref, y_ref, y_swap1_ref, y_swap2_ref,
    stats_ref, back_ref, gain_ref, two_ref, stash_ref,
    keep_ref, give_ref, halves_ref, dgain_ref, dbias_ref,
    ext, grad, taken, sems,
):
    rank, live, even = position(cumulative_ref)
    total = cumulative_ref[stats_ref.shape[0]].astype(F32)
    width = y_ref.shape[1]
    codes = ring.codes(rank)

    def make_dy():
        mean, scale = norm_stats(stats_ref, cumulative_ref)

        def part(dz, y):
            return norm_back(dz, (y - mean) * scale, scale, gain_ref[...], back_ref, total)

        dz_before, dz_after = sides(swap1_ref[...], swap2_ref[...], even)
        y_before, y_after = sides(y_swap1_ref[:HALO, :], y_swap2_ref[:HALO, :], even)
        dy, dgain, dbias = part(dz_ref[...], y_ref[...])
        dgain_ref[...] = dgain
        dbias_ref[...] = dbias
        place(ext, part(dz_before, y_before)[0], dy, part(dz_after, y_after)[0], live)
        high, low = split(ext[...])
        halves_ref[:, :width] = high
        halves_ref[:, width:] = low
        return dy

    def store(k, value):
        ring.store(grad, codes, k * (value.shape[0] // 8), value)

    kernel_grads(make_dy, stash_ref, taken, sems, store)
    keep_ref[...] = jnp.where(even, two_ref[...], grad[...])
    give_ref[...] = jnp.where(even, grad[...], two_ref[...])


def back_one_kernel(
    block, halves_ref, target_ref, dpre_ref, kernel_ref, *refs
):
    dx_ref, zero_ref, result, sem = refs[-4:]
    rows = BLOCK * block
    dx = scatter_conv(halves_ref, target_ref, kernel_ref, (block,))
    result[...] = dx + dpre_ref[rows : rows + BLOCK, :]
    store = pltpu.make_async_copy(result, dx_ref.at[pl.ds(rows, BLOCK)], sem)
    store.start()
    zero_ref[...] = jnp.zeros_like(zero_ref)
    store.wait()


def finish_kernel(ring, *refs):
    count = len(ring.orders)
    low, high, low_other, high_other = (refs[i * count : (i + 1) * count] for i in range(4))
    one_ref, two_ref, sems = refs[4 * count :]
    rank = lax.axis_index("vox")
    codes = ring.codes(rank)
    half = ring.chips // 2

    def spread(pieces, ref, sem):
        for part, halves in enumerate(zip(*pieces)):
            for block in range(ring.chips):
                size = ring.sizes[part]
                at = ring.starts[part] + (block ^ codes[part]) * size
                pltpu.make_async_copy(
                    halves[block // half].at[pl.ds(block % half * size, size)],
                    ref.at[pl.ds(at, size)],
                    sem,
                ).start()

    def finish(own_ref, other_ref):
        spread((low, high), own_ref, sems.at[0])
        spread((low_other, high_other), other_ref, sems.at[1])
        for i, ref in enumerate((own_ref, other_ref)):
            pltpu.make_async_copy(ref, ref, sems.at[i]).wait()

    @pl.when(rank % 2 == 0)
    def _():
        finish(two_ref, one_ref)

    @pl.when(rank % 2 == 1)
    def _():
        finish(one_ref, two_ref)


def run(body, cumulative, arrays, outs, scratch, flops=0, limit=28, aliases=None):
    plain = pl.BlockSpec(memory_space=pltpu.VMEM)
    there = pl.BlockSpec(memory_space=pltpu.MemorySpace.HBM)
    shapes, out_specs = [], []
    for out in outs:
        if out[0] == "near":
            shapes.append(pltpu.VMEM(*out[1:]))
            out_specs.append(plain)
        elif out[0] == "here":
            shapes.append(jax.ShapeDtypeStruct(*out[1:]))
            out_specs.append(plain)
        elif out[0] == "far":
            shapes.append(pltpu.MemorySpace.HBM(*out[1:]))
            out_specs.append(there)
        else:
            shapes.append(jax.ShapeDtypeStruct(out, F32))
            out_specs.append(plain)
    any_space = pl.BlockSpec(memory_space=pl.ANY)
    operands, specs = [], []
    if cumulative is not None:
        operands.append(pltpu.with_memory_space_constraint(cumulative, pltpu.MemorySpace.HBM))
        specs.append(pl.BlockSpec(memory_space=pltpu.SMEM))
    for array in arrays:
        how, array = array if isinstance(array, tuple) else ("near", array)
        specs.append({"near": plain, "here": plain, "far": there, "any": any_space}[how])
        if how in ("near", "far"):
            space = pltpu.VMEM if how == "near" else pltpu.MemorySpace.HBM
            array = pltpu.with_memory_space_constraint(array, space)
        operands.append(array)
    return pl.pallas_call(
        body,
        in_specs=specs,
        out_specs=out_specs,
        out_shape=shapes,
        scratch_shapes=scratch,
        input_output_aliases=aliases or {},
        cost_estimate=pl.CostEstimate(flops=flops, bytes_accessed=2**20, transcendentals=0),
        compiler_params=pltpu.CompilerParams(vmem_limit_bytes=limit * 2**20),
    )(*operands)


def sum_chips(ring, pairs, swap_chips, swap_cores, beside, zero):
    stages = len(ring.orders[0])
    for stage in range(stages):
        wider = []
        for (a, b), order in zip(pairs, ring.orders):
            half = a.shape[0] // 2
            sent = a[half:] + b[half:]
            if zero is not None:
                sent = sent + zero
            wider.append((a[:half] + b[:half], swap_chips(sent, order[stage])))
        pairs = wider
        zero = beside(sent) if stage in BESIDE[0] else None
    pieces = [a + b for a, b in pairs]
    for stage in reversed(range(1, stages)):
        got = [swap_chips(piece, order[stage]) for piece, order in zip(pieces, ring.orders)]
        zero = beside(pieces[-1]) if stage in BESIDE[1] else None
        pieces = [jnp.concatenate(both, 0) for both in zip(pieces, got)]
        if zero is not None:
            pieces = [piece + zero for piece in pieces]
    highs = [swap_chips(piece, order[0]) for piece, order in zip(pieces, ring.orders)]
    zero = beside(pieces[-1])
    highs[LATE] = highs[LATE] + zero
    return (*pieces, *highs, *map(swap_cores, pieces), *map(swap_cores, highs))


def per_device(
    features,
    kernel_one,
    gain_one,
    bias_one,
    kernel_two,
    gain_two,
    bias_two,
    cotangent,
    cumulative,
    neighbours,
):
    rank = lax.axis_index("vox")
    count = cumulative.shape[0] - 1
    ends = lax.dynamic_slice(cumulative, (rank,), (2,), allow_negative_indices=False)
    tail = ends[1] - ends[0] - HALO
    rows, width = features.shape
    offsets = neighbours.shape[0]
    even = rank % 2 == 0
    gain_one, bias_one = gain_one[None], bias_one[None]
    gain_two, bias_two = gain_two[None], bias_two[None]

    def swap(first, second):
        within = [(i, i ^ 1) for i in range(count)]
        across = [(i, i + 1) for i in range(1, count - 1, 2)]
        across = across + [(j, i) for i, j in across]
        return (lax.ppermute(first, "vox", within), lax.ppermute(second, "vox", across))

    def spread(stats):
        return lax.all_to_all(stats, "vox", 0, 0)

    def more(start):
        def part(array, shape, where):
            return lax.dynamic_slice(array, where, shape, allow_negative_indices=False)

        zero = jnp.zeros_like(start)
        return jnp.concatenate(
            [
                part(cotangent, (HALO, width), (start, zero)),
                part(neighbours, (offsets, HALO), (zero, start)).astype(F32),
            ],
            0,
        )

    ext_shape = (rows + 2 * HALO, width)
    stats_shape = (count, 2, width)
    edge = (HALO, width)
    wide_edge = (2 * HALO + offsets, width)
    vector = (1, width)
    turned_rows = -(-offsets // 8) * 8
    taken = (offsets, 2 * width, rows)
    halves = (ext_shape[0], 2 * width)
    conv_scratch = [
        pltpu.VMEM(ext_shape, F32),
        pltpu.VMEM((offsets, width, width), F32),
        pltpu.VMEM(taken, BF16),
        pltpu.VMEM(ext_shape[::-1], F32),
        pltpu.VMEM(halves[::-1], BF16),
        pltpu.SemaphoreType.DMA((4,)),
    ]
    grad_scratch = [pltpu.VMEM(taken, BF16), pltpu.SemaphoreType.DMA((len(CHUNKS) - 1,))]
    x_edges = swap(
        *run(
            pack_kernel,
            cumulative,
            (("far", features),),
            (edge, edge),
            [pltpu.VMEM(edge, F32), pltpu.VMEM((HALO + 8, width), F32), pltpu.SemaphoreType.DMA((2,))],
        )
    )
    mores = (more(jnp.where(even, tail, 0)), more(jnp.where(even, 0, tail)))
    ring = Ring(count, offsets * width // 8)
    grad = (ring.padded, 8, width)
    work = 2 * offsets * rows * width * width * 4

    def move(piece, pairs):
        return lax.ppermute(piece, "vox", pairs)

    def near(shape, kind=F32):
        return ("near", shape, kind)

    y1, swap1, swap2, stats, stash1 = run(
        first_kernel,
        cumulative,
        (*x_edges, *mores, ("far", features), ("far", neighbours), ("far", kernel_one)),
        (near((rows, width)), wide_edge, wide_edge, stats_shape, ("far", taken, BF16)),
        [
            pltpu.VMEM(neighbours.shape, jnp.int32),
            pltpu.SemaphoreType.DMA((2,)),
            *conv_scratch,
        ],
        flops=3 * work,
    )
    y1_edges = swap(swap1, swap2)
    stats1 = spread(stats)
    y2, swap1, swap2, stats, stash2, target, later_target = run(
        second_kernel,
        cumulative,
        (y1, *y1_edges, stats1, gain_one, bias_one, neighbours, ("far", kernel_two)),
        (
            near((rows, width)), edge, edge, stats_shape, ("far", taken, BF16),
            near((turned_rows, ext_shape[0]), jnp.int32),
            ("far", (turned_rows, ext_shape[0]), jnp.int32),
        ),
        [
            pltpu.VMEM((ext_shape[0], turned_rows), jnp.int32),
            pltpu.SemaphoreType.DMA,
            *conv_scratch,
        ],
        flops=3 * work,
    )
    y2_edges = swap(swap1, swap2)
    stats2 = spread(stats)
    output, dz2, unit2, stats = run(
        middle_kernel,
        cumulative,
        (
            y2, *y2_edges, stats2, gain_two, bias_two, features, *x_edges, *y1_edges, cotangent,
        ),
        ((rows, width), near(ext_shape), near(ext_shape), stats_shape),
        [],
    )
    back2 = spread(stats)
    dy2, dpre, dz1, swap1, swap2, stats, dgain_two, dbias_two = run(
        back_two_kernel,
        cumulative,
        (
            dz2, unit2, stats2, back2, gain_two, target, y1, stats1, gain_one, bias_one,
            kernel_two,
        ),
        (
            ("far", (rows, width), F32), ("far", (rows, width), F32), near((rows, width)), edge,
            edge, stats_shape, vector, vector,
        ),
        [
            pltpu.VMEM(halves, BF16),
            pltpu.VMEM((2, rows, width), F32),
            pltpu.SemaphoreType.DMA((2,)),
        ],
        flops=3 * work,
    )
    dz_edges = swap(swap1, swap2)
    back1 = spread(stats)
    (two,) = run(
        functools.partial(grad_two_kernel, ring),
        None,
        (("far", dy2), ("far", stash2)),
        (near(grad),),
        [pltpu.VMEM((rows, width), F32), pltpu.SemaphoreType.DMA, *grad_scratch],
        flops=work,
    )
    keep, give, halves_one, dgain_one, dbias_one = run(
        functools.partial(grad_one_kernel, ring),
        cumulative,
        (
            dz1, *dz_edges, y1, *y1_edges, stats1, back1, gain_one, two, ("far", stash1),
        ),
        (grad, grad, near(halves, BF16), vector, vector),
        [pltpu.VMEM(ext_shape, F32), pltpu.VMEM(grad, F32), *grad_scratch],
        flops=work,
    )
    theirs = move(give, [(i, i ^ 1) for i in range(count)])
    dx = None
    blocks = list(range(rows // BLOCK))

    def beside(sent):
        nonlocal dx
        block = blocks.pop(0)
        arrays = (halves_one, later_target, dpre, kernel_one, ("any", sent))
        dx, zero = run(
            functools.partial(back_one_kernel, block),
            None,
            arrays if dx is None else (*arrays, ("far", dx)),
            (("far", (rows, width), F32), (8, width)),
            [pltpu.VMEM((BLOCK, width), F32), pltpu.SemaphoreType.DMA],
            flops=3 * work // (rows // BLOCK),
            aliases=None if dx is None else {len(arrays): 0},
        )
        return zero

    def part(array, w):
        return array[ring.starts[w] : ring.starts[w + 1]]

    sums = sum_chips(
        ring,
        [(part(keep, w), part(theirs, w)) for w in range(len(ring.orders))],
        lambda piece, bit: move(piece, [(i, i ^ (1 << bit)) for i in range(count)]),
        lambda piece: move(piece, [(i, i ^ 1) for i in range(count)]),
        beside,
        beside(give),
    )
    grads = run(
        functools.partial(finish_kernel, ring),
        None,
        [("any", piece) for piece in sums],
        (("far", grad, F32), ("far", grad, F32)),
        [pltpu.SemaphoreType.DMA((2,))],
    )
    dkernel_one, dkernel_two = (
        array[: ring.tiles].reshape(offsets, width, width) for array in grads
    )
    return (
        output,
        dx,
        dkernel_one,
        dkernel_two,
        dgain_one[0],
        dbias_one[0],
        dgain_two[0],
        dbias_two[0],
    )


def solution(mesh):
    return jax.shard_map(
        per_device,
        mesh=mesh,
        in_specs=(
            P("vox", None),
            P(),
            P(),
            P(),
            P(),
            P(),
            P(),
            P("vox", None),
            P(),
            P(None, "vox"),
        ),
        out_specs=(P("vox", None), P("vox", None), P(), P(), P(), P(), P(), P()),
        check_vma=False,
    )
```

```python
import functools

import jax
import jax.numpy as jnp
from jax import lax
from jax.experimental import pallas as pl
from jax.experimental.pallas import tpu as pltpu
from jax.sharding import PartitionSpec as P

HALO = 128
BLOCK = 256
SPAN = BLOCK + 2 * HALO
EPS = 1e-05
SHARE = 9
BESIDE = ((0,), (1,))
LATE = 2
CHUNKS = (0.0, 0.25, 0.65, 1.0)
F32 = jnp.float32
BF16 = jnp.bfloat16


def split(values):
    high = values.astype(BF16)
    low = (values - high.astype(F32)).astype(BF16)
    return (high, low)


def silu_slope(values):
    sigma = jax.nn.sigmoid(values)
    return sigma * (1.0 + values * (1.0 - sigma))


def position(cumulative_ref):
    rank = lax.axis_index("vox")
    return (rank, cumulative_ref[rank + 1] - cumulative_ref[rank], rank % 2 == 0)


def sides(first, second, even):
    return (jnp.where(even, second, first), jnp.where(even, first, second))


def row_mask(rows, live):
    return lax.broadcasted_iota(jnp.int32, (rows, 1), 0) < live


def place(ref, before, own, after, live):
    rows = own.shape[0]
    ref[:HALO, :] = before
    ref[HALO : HALO + rows, :] = own
    ref[HALO + rows :, :] = jnp.zeros((HALO, own.shape[1]), F32)
    ref[pl.ds(HALO + live, HALO), :] = after


def one_hot(index, rows, axis):
    shape = (SPAN, rows) if axis == 0 else (rows, index.shape[1])
    return (index == lax.broadcasted_iota(jnp.int32, shape, 0)).astype(F32).astype(BF16)


def gather_conv(ext, index_ref, kernel_ref, stash_ref, matrices, taken, turned, halves, sems, live):
    offsets, width = kernel_ref.shape[0], kernel_ref.shape[2]
    rows = index_ref.shape[1]
    chunks = sems.shape[0] - 1
    fetch = pltpu.make_async_copy(kernel_ref, matrices, sems.at[chunks])
    fetch.start()
    for j in range(ext.shape[0] // HALO):
        at = slice(HALO * j, HALO * (j + 1))
        turned[:, at] = ext[at, :].T
        halves[:width, at], halves[width:, at] = split(turned[:, at])
    index = index_ref[...]
    index = jnp.where(index >= HALO + rows, index - rows + live, index)

    def by_product(k, start):
        hit = one_hot(index[k : k + 1, start : start + BLOCK] - start, BLOCK, 0)
        window = halves[:, start : start + SPAN]
        got = jnp.dot(window, hit, preferred_element_type=F32)
        taken[k, :, start : start + BLOCK] = got.astype(BF16)

    def by_lanes(k, start):
        place = index[k : k + 1, start : start + HALO] - start
        piece = jnp.broadcast_to(lax.shift_right_arithmetic(place, 7), (width, HALO))
        lane = jnp.broadcast_to(lax.bitwise_and(place, HALO - 1), (width, HALO))
        total = jnp.zeros((width, HALO), F32)
        for p in range(2, -1, -1):
            block = turned[:, start + HALO * p : start + HALO * (p + 1)]
            got = jnp.take_along_axis(block, lane, axis=1, mode="promise_in_bounds")
            total = jnp.where(piece == p, got, total)
        at = slice(start, start + HALO)
        taken[k, :width, at], taken[k, width:, at] = split(total)

    ends = [offsets * c // chunks for c in range(chunks + 1)]
    stashes = []
    for c in range(chunks):
        for k in range(ends[c], ends[c + 1]):
            for start in range(0, rows // 2, BLOCK):
                by_product(k, start)
            for start in range(rows // 2, rows, HALO):
                by_lanes(k, start)
        part = pl.ds(ends[c], ends[c + 1] - ends[c])
        stashes.append(pltpu.make_async_copy(taken.at[part], stash_ref.at[part], sems.at[c]))
        stashes[c].start()
    fetch.wait()
    total = jnp.zeros((2 * width, rows), F32)
    for k in range(offsets):
        both = jnp.concatenate(split(matrices[k].T), 0)
        total = total + jnp.dot(
            jnp.concatenate([both, both], 1), taken[k], preferred_element_type=F32
        )
    total = total[:width] + total[width:]
    for stash in stashes:
        stash.wait()
    return jnp.concatenate(
        [total[:, HALO * j : HALO * (j + 1)].T for j in range(rows // HALO)], 0
    )


def scatter_conv(halves, target_ref, kernel_ref, blocks):
    offsets, width = kernel_ref.shape[0], kernel_ref.shape[2]
    total = jnp.zeros((len(blocks) * BLOCK, 2 * width), F32)
    for k in range(offsets):
        spread = []
        for b in blocks:
            index = target_ref[k : k + 1, BLOCK * b : BLOCK * b + SPAN] - BLOCK * b
            window = halves[BLOCK * b : BLOCK * b + SPAN, :]
            got = jnp.dot(one_hot(index, BLOCK, 1), window, preferred_element_type=F32)
            spread.append(jnp.concatenate(split(got[:, :width] + got[:, width:]), 1))
        tall = jnp.concatenate(split(kernel_ref[k]), 0)
        total = total + lax.dot_general(
            jnp.concatenate(spread, 0),
            jnp.concatenate([tall, tall], 1),
            (((1,), (1,)), ((), ())),
            preferred_element_type=F32,
        )
    return total[:, :width] + total[:, width:]


def kernel_grads(make_dy, stash_ref, taken, sems, store):
    offsets, width = taken.shape[0], taken.shape[1] // 2
    ends = [round(offsets * e) for e in CHUNKS]
    fetches = []
    for c, (start, end) in enumerate(zip(ends, ends[1:])):
        part = pl.ds(start, end - start)
        fetches.append(pltpu.make_async_copy(stash_ref.at[part], taken.at[part], sems.at[c]))
        fetches[c].start()
    wide = jnp.concatenate(split(make_dy()), 1)
    for c, (start, end) in enumerate(zip(ends, ends[1:])):
        fetches[c].wait()
        for k in range(start, end):
            outer = jnp.dot(taken[k], wide, preferred_element_type=F32)
            outer = outer[:, :width] + outer[:, width:]
            store(k, outer[:width] + outer[width:])


class Ring:
    def __init__(self, count, tiles):
        bits = list(range(1, count.bit_length() - 1))
        x, y, z = bits[:3]
        self.orders = [[*order, *bits[3:]] for order in ((x, z, y), (y, x, z), (z, y, x))]
        self.chips = count // 2
        self.tiles = tiles
        share = -(-tiles // self.chips)
        last = share * SHARE // 27
        first = (share - last + 1) // 2
        self.sizes = [first, share - last - first, last]
        self.starts = [self.chips * sum(self.sizes[:w]) for w in range(4)]
        self.padded = self.starts[3]

    def codes(self, rank):
        return [sum(((rank >> bit) & 1) << (len(order) - 1 - s) for s, bit in enumerate(order)) for order in self.orders]

    def store(self, ref, codes, first, value):
        for j in range(value.shape[0] // 8):
            part = sum(first + j >= start for start in self.starts[1:3])
            block, tile = divmod(first + j - self.starts[part], self.sizes[part])
            at = self.starts[part] + (block ^ codes[part]) * self.sizes[part] + tile
            ref[at] = value[8 * j : 8 * (j + 1), :]


def norm_stats(gathered_ref, cumulative_ref):
    count = gathered_ref.shape[0]
    total = cumulative_ref[count].astype(F32)
    mean = jnp.sum(gathered_ref[:, 0:1, :], 0) / total

    def step(d, spread):
        live = (cumulative_ref[d + 1] - cumulative_ref[d]).astype(F32)
        own = gathered_ref[d, 0:1, :] / live - mean
        return spread + gathered_ref[d, 1:2, :] + live * own * own

    spread = lax.fori_loop(0, count, step, jnp.zeros_like(mean))
    return (mean, lax.rsqrt(spread / total + EPS))


def share(stats_ref, first, second):
    both = jnp.concatenate([first, second], 0)
    stats_ref[...] = jnp.broadcast_to(both[None], stats_ref.shape)


def conv_stats(y, mask, live, stats_ref):
    first = jnp.sum(y, 0, keepdims=True)
    centred = jnp.where(mask, y - first / live.astype(F32), 0.0)
    share(stats_ref, first, jnp.sum(centred * centred, 0, keepdims=True))


def edges(first_ref, second_ref, ref, live, even):
    first_ref[:HALO, :] = ref[pl.ds(jnp.where(even, live - HALO, 0), HALO), :]
    second_ref[:HALO, :] = ref[pl.ds(jnp.where(even, 0, live - HALO), HALO), :]


def targets(target_ref, index_ref, before, after, live, rank, count, spread):
    rows = index_ref.shape[1]
    offsets = index_ref.shape[0]
    own = index_ref[...]
    own = jnp.where((own >= HALO) & (own < HALO + rows), own - HALO, -1)
    before = before.astype(jnp.int32) - (HALO + rows)
    before = jnp.where((before >= 0) & (rank > 0), before, -1)
    after = after.astype(jnp.int32)
    after = jnp.where(
        (after >= 0) & (after < HALO) & (rank < count - 1), after + live - HALO, -1
    )
    fill = jnp.full((target_ref.shape[0] - offsets, HALO), -1, jnp.int32)

    def turn(block):
        return jnp.concatenate([block, fill], 0).T

    spread[:HALO, :] = turn(before)
    for j in range(rows // HALO):
        spread[HALO * (j + 1) : HALO * (j + 2), :] = turn(own[:, HALO * j : HALO * (j + 1)])
    spread[HALO + rows :, :] = jnp.full((HALO, target_ref.shape[0]), -1, jnp.int32)
    spread[pl.ds(HALO + live, HALO), :] = turn(after)
    for j in range(target_ref.shape[1] // HALO):
        target_ref[:, HALO * j : HALO * (j + 1)] = spread[HALO * j : HALO * (j + 1), :].T


def pack_kernel(cumulative_ref, x_ref, first_ref, second_ref, head, near_tail, sems):
    _, live, even = position(cumulative_ref)
    tail = live - HALO
    start = pl.multiple_of(jnp.minimum(tail // 8 * 8, x_ref.shape[0] - near_tail.shape[0]), 8)
    fetches = [
        pltpu.make_async_copy(x_ref.at[pl.ds(0, HALO)], head, sems.at[0]),
        pltpu.make_async_copy(x_ref.at[pl.ds(start, near_tail.shape[0])], near_tail, sems.at[1]),
    ]
    for fetch in fetches:
        fetch.start()
    for fetch in fetches:
        fetch.wait()
    last = near_tail[pl.ds(tail - start, HALO), :]
    first_ref[...] = jnp.where(even, last, head[...])
    second_ref[...] = jnp.where(even, head[...], last)


def first_kernel(
    cumulative_ref, before_ref, after_ref, more1_ref, more2_ref, x_ref, neighbours_ref, kernel_ref,
    y_ref, swap1_ref, swap2_ref, stats_ref, stash_ref,
    index_ref, fetched, ext, *scratch,
):
    rows, width = x_ref.shape
    fetches = [
        pltpu.make_async_copy(x_ref, ext.at[pl.ds(HALO, rows)], fetched.at[0]),
        pltpu.make_async_copy(neighbours_ref, index_ref, fetched.at[1]),
    ]
    for fetch in fetches:
        fetch.start()
    _, live, even = position(cumulative_ref)
    before, after = sides(before_ref[...], after_ref[...], even)
    ext[:HALO, :] = before
    ext[HALO + rows :, :] = jnp.zeros((HALO, width), F32)
    for fetch in fetches:
        fetch.wait()
    ext[pl.ds(HALO + live, HALO), :] = after
    y = gather_conv(ext, index_ref, kernel_ref, stash_ref, *scratch, live)
    y_ref[...] = y
    conv_stats(y, row_mask(rows, live), live, stats_ref)
    edges(swap1_ref, swap2_ref, y_ref, live, even)
    swap1_ref[HALO:, :] = more1_ref[...]
    swap2_ref[HALO:, :] = more2_ref[...]


def second_kernel(
    cumulative_ref, y1_ref, swapped1_ref, swapped2_ref, gathered_ref, gain_ref, bias_ref,
    index_ref, kernel_ref,
    y_ref, swap1_ref, swap2_ref, stats_ref, stash_ref, target_ref, later_ref,
    spread, sent, ext, *scratch,
):
    rank, live, even = position(cumulative_ref)
    count = gathered_ref.shape[0]
    mean, scale = norm_stats(gathered_ref, cumulative_ref)
    rows = y1_ref.shape[0]
    mask = row_mask(rows, live)

    def act(y):
        a = (y - mean) * scale * gain_ref[...] + bias_ref[...]
        return a * jax.nn.sigmoid(a)

    own = jnp.where(mask, act(y1_ref[...]), 0.0)
    before, after = sides(swapped1_ref[:HALO, :], swapped2_ref[:HALO, :], even)
    before = jnp.where(rank > 0, act(before), 0.0)
    after = jnp.where(rank < count - 1, act(after), 0.0)
    place(ext, before, own, after, live)
    before, after = sides(swapped1_ref[2 * HALO :, :], swapped2_ref[2 * HALO :, :], even)
    targets(target_ref, index_ref, before, after, live, rank, count, spread)
    later = pltpu.make_async_copy(target_ref, later_ref, sent)
    later.start()
    y = gather_conv(ext, index_ref, kernel_ref, stash_ref, *scratch, live)
    y_ref[...] = y
    conv_stats(y, mask, live, stats_ref)
    edges(swap1_ref, swap2_ref, y_ref, live, even)
    later.wait()


def middle_kernel(
    cumulative_ref, y_ref, y_swap1_ref, y_swap2_ref, gathered_ref, gain_ref, bias_ref,
    x_ref, x_swap1_ref, x_swap2_ref, swapped1_ref, swapped2_ref, cotangent_ref,
    out_ref, dz_ref, unit_ref, stats_ref,
):
    _, live, even = position(cumulative_ref)
    mean, scale = norm_stats(gathered_ref, cumulative_ref)
    mask = row_mask(x_ref.shape[0], live)

    def part(y, x, cotangent):
        unit = (y - mean) * scale
        pre = unit * gain_ref[...] + bias_ref[...] + x
        return (unit, pre, cotangent * silu_slope(pre))

    unit, pre, dz = part(y_ref[...], x_ref[...], cotangent_ref[...])
    dz = jnp.where(mask, dz, 0.0)
    out_ref[...] = jnp.where(mask, pre * jax.nn.sigmoid(pre), 0.0)
    share(
        stats_ref, jnp.sum(dz, 0, keepdims=True), jnp.sum(dz * unit, 0, keepdims=True)
    )
    y_before, y_after = sides(y_swap1_ref[...], y_swap2_ref[...], even)
    x_before, x_after = sides(x_swap1_ref[...], x_swap2_ref[...], even)
    more = slice(HALO, 2 * HALO)
    before, after = sides(swapped1_ref[more, :], swapped2_ref[more, :], even)
    unit_b, _, dz_b = part(y_before, x_before, before)
    unit_a, _, dz_a = part(y_after, x_after, after)
    place(dz_ref, dz_b, dz, dz_a, live)
    place(unit_ref, unit_b, unit, unit_a, live)


def norm_back(dz, unit, scale, gain, gathered_ref, total):
    dbias = jnp.sum(gathered_ref[:, 0:1, :], 0)
    dgain = jnp.sum(gathered_ref[:, 1:2, :], 0)
    slope = scale * gain
    return (slope * dz - slope * dbias / total - unit * (slope * dgain / total), dgain, dbias)


def back_two_kernel(
    cumulative_ref, dz_ref, unit_ref, stats2_ref, back_ref, gain2_ref, target_ref,
    y1_ref, stats1_ref, gain1_ref, bias1_ref, kernel_ref,
    dy_ref, dpre_ref, dz1_ref, swap1_ref, swap2_ref, stats_ref, dgain_ref, dbias_ref,
    halves, own, sent,
):
    _, live, even = position(cumulative_ref)
    count = stats1_ref.shape[0]
    total = cumulative_ref[count].astype(F32)
    rows, width = y1_ref.shape
    _, scale2 = norm_stats(stats2_ref, cumulative_ref)
    dy, dgain, dbias = norm_back(
        dz_ref[...], unit_ref[...], scale2, gain2_ref[...], back_ref, total
    )
    dgain_ref[...] = dgain
    dbias_ref[...] = dbias
    mask = row_mask(rows, live)
    own[0] = dy[HALO : HALO + rows]
    own[1] = jnp.where(mask, dz_ref[HALO : HALO + rows, :], 0.0)
    later = [
        pltpu.make_async_copy(own.at[i], ref, sent.at[i]) for i, ref in enumerate((dy_ref, dpre_ref))
    ]
    for copy in later:
        copy.start()
    high, low = split(dy)
    halves[:, :width] = high
    halves[:, width:] = low
    dhidden = scatter_conv(halves, target_ref, kernel_ref, range(rows // BLOCK))
    mean1, scale1 = norm_stats(stats1_ref, cumulative_ref)
    unit1 = (y1_ref[...] - mean1) * scale1
    slope = silu_slope(unit1 * gain1_ref[...] + bias1_ref[...])
    dz1 = jnp.where(mask, dhidden * slope, 0.0)
    dz1_ref[...] = dz1
    share(stats_ref, jnp.sum(dz1, 0, keepdims=True), jnp.sum(dz1 * unit1, 0, keepdims=True))
    edges(swap1_ref, swap2_ref, dz1_ref, live, even)
    for copy in later:
        copy.wait()


def grad_two_kernel(ring, dy_ref, stash_ref, grad_ref, own_dy, sent, taken, sems):
    fetch = pltpu.make_async_copy(dy_ref, own_dy, sent)
    fetch.start()
    codes = ring.codes(lax.axis_index("vox"))

    def store(k, value):
        ring.store(grad_ref, codes, k * (value.shape[0] // 8), value)

    def make_dy():
        fetch.wait()
        return own_dy[...]

    kernel_grads(make_dy, stash_ref, taken, sems, store)


def grad_one_kernel(
    ring,
    cumulative_ref, dz_ref, swap1_ref, swap2_ref, y_ref, y_swap1_ref, y_swap2_ref,
    stats_ref, back_ref, gain_ref, two_ref, stash_ref,
    keep_ref, give_ref, halves_ref, dgain_ref, dbias_ref,
    ext, grad, taken, sems,
):
    rank, live, even = position(cumulative_ref)
    total = cumulative_ref[stats_ref.shape[0]].astype(F32)
    width = y_ref.shape[1]
    codes = ring.codes(rank)

    def make_dy():
        mean, scale = norm_stats(stats_ref, cumulative_ref)

        def part(dz, y):
            return norm_back(dz, (y - mean) * scale, scale, gain_ref[...], back_ref, total)

        dz_before, dz_after = sides(swap1_ref[...], swap2_ref[...], even)
        y_before, y_after = sides(y_swap1_ref[:HALO, :], y_swap2_ref[:HALO, :], even)
        dy, dgain, dbias = part(dz_ref[...], y_ref[...])
        dgain_ref[...] = dgain
        dbias_ref[...] = dbias
        place(ext, part(dz_before, y_before)[0], dy, part(dz_after, y_after)[0], live)
        high, low = split(ext[...])
        halves_ref[:, :width] = high
        halves_ref[:, width:] = low
        return dy

    def store(k, value):
        ring.store(grad, codes, k * (value.shape[0] // 8), value)

    kernel_grads(make_dy, stash_ref, taken, sems, store)
    keep_ref[...] = jnp.where(even, two_ref[...], grad[...])
    give_ref[...] = jnp.where(even, grad[...], two_ref[...])


def back_one_kernel(
    block, halves_ref, target_ref, dpre_ref, kernel_ref, *refs
):
    dx_ref, zero_ref, result, sem = refs[-4:]
    rows = BLOCK * block
    dx = scatter_conv(halves_ref, target_ref, kernel_ref, (block,))
    result[...] = dx + dpre_ref[rows : rows + BLOCK, :]
    store = pltpu.make_async_copy(result, dx_ref.at[pl.ds(rows, BLOCK)], sem)
    store.start()
    zero_ref[...] = jnp.zeros_like(zero_ref)
    store.wait()


def finish_kernel(ring, *refs):
    count = len(ring.orders)
    low, high, low_other, high_other = (refs[i * count : (i + 1) * count] for i in range(4))
    one_ref, two_ref, sems = refs[4 * count :]
    rank = lax.axis_index("vox")
    codes = ring.codes(rank)
    half = ring.chips // 2

    def spread(pieces, ref, sem):
        for part, halves in enumerate(zip(*pieces)):
            for block in range(ring.chips):
                size = ring.sizes[part]
                at = ring.starts[part] + (block ^ codes[part]) * size
                pltpu.make_async_copy(
                    halves[block // half].at[pl.ds(block % half * size, size)],
                    ref.at[pl.ds(at, size)],
                    sem,
                ).start()

    def finish(own_ref, other_ref):
        spread((low, high), own_ref, sems.at[0])
        spread((low_other, high_other), other_ref, sems.at[1])
        for i, ref in enumerate((own_ref, other_ref)):
            pltpu.make_async_copy(ref, ref, sems.at[i]).wait()

    @pl.when(rank % 2 == 0)
    def _():
        finish(two_ref, one_ref)

    @pl.when(rank % 2 == 1)
    def _():
        finish(one_ref, two_ref)


def run(body, cumulative, arrays, outs, scratch, flops=0, limit=28, aliases=None):
    plain = pl.BlockSpec(memory_space=pltpu.VMEM)
    there = pl.BlockSpec(memory_space=pltpu.MemorySpace.HBM)
    shapes, out_specs = [], []
    for out in outs:
        if out[0] == "near":
            shapes.append(pltpu.VMEM(*out[1:]))
            out_specs.append(plain)
        elif out[0] == "here":
            shapes.append(jax.ShapeDtypeStruct(*out[1:]))
            out_specs.append(plain)
        elif out[0] == "far":
            shapes.append(pltpu.MemorySpace.HBM(*out[1:]))
            out_specs.append(there)
        else:
            shapes.append(jax.ShapeDtypeStruct(out, F32))
            out_specs.append(plain)
    any_space = pl.BlockSpec(memory_space=pl.ANY)
    operands, specs = [], []
    if cumulative is not None:
        operands.append(pltpu.with_memory_space_constraint(cumulative, pltpu.MemorySpace.HBM))
        specs.append(pl.BlockSpec(memory_space=pltpu.SMEM))
    for array in arrays:
        how, array = array if isinstance(array, tuple) else ("near", array)
        specs.append({"near": plain, "here": plain, "far": there, "any": any_space}[how])
        if how in ("near", "far"):
            space = pltpu.VMEM if how == "near" else pltpu.MemorySpace.HBM
            array = pltpu.with_memory_space_constraint(array, space)
        operands.append(array)
    return pl.pallas_call(
        body,
        in_specs=specs,
        out_specs=out_specs,
        out_shape=shapes,
        scratch_shapes=scratch,
        input_output_aliases=aliases or {},
        cost_estimate=pl.CostEstimate(flops=flops, bytes_accessed=2**20, transcendentals=0),
        compiler_params=pltpu.CompilerParams(vmem_limit_bytes=limit * 2**20),
    )(*operands)


def sum_chips(ring, pairs, swap_chips, swap_cores, beside, zero):
    stages = len(ring.orders[0])
    for stage in range(stages):
        wider = []
        for (a, b), order in zip(pairs, ring.orders):
            half = a.shape[0] // 2
            sent = a[half:] + b[half:]
            if zero is not None:
                sent = sent + zero
            wider.append((a[:half] + b[:half], swap_chips(sent, order[stage])))
        pairs = wider
        zero = beside(sent) if stage in BESIDE[0] else None
    pieces = [a + b for a, b in pairs]
    for stage in reversed(range(1, stages)):
        got = [swap_chips(piece, order[stage]) for piece, order in zip(pieces, ring.orders)]
        zero = beside(pieces[-1]) if stage in BESIDE[1] else None
        pieces = [jnp.concatenate(both, 0) for both in zip(pieces, got)]
        if zero is not None:
            pieces = [piece + zero for piece in pieces]
    highs = [swap_chips(piece, order[0]) for piece, order in zip(pieces, ring.orders)]
    zero = beside(pieces[-1])
    highs[LATE] = highs[LATE] + zero
    return (*pieces, *highs, *map(swap_cores, pieces), *map(swap_cores, highs))


def per_device(
    features,
    kernel_one,
    gain_one,
    bias_one,
    kernel_two,
    gain_two,
    bias_two,
    cotangent,
    cumulative,
    neighbours,
):
    rank = lax.axis_index("vox")
    count = cumulative.shape[0] - 1
    ends = lax.dynamic_slice(cumulative, (rank,), (2,), allow_negative_indices=False)
    tail = ends[1] - ends[0] - HALO
    rows, width = features.shape
    offsets = neighbours.shape[0]
    even = rank % 2 == 0
    gain_one, bias_one = gain_one[None], bias_one[None]
    gain_two, bias_two = gain_two[None], bias_two[None]

    def swap(first, second):
        within = [(i, i ^ 1) for i in range(count)]
        across = [(i, i + 1) for i in range(1, count - 1, 2)]
        across = across + [(j, i) for i, j in across]
        return (lax.ppermute(first, "vox", within), lax.ppermute(second, "vox", across))

    def spread(stats):
        return lax.all_to_all(stats, "vox", 0, 0)

    def more(start):
        def part(array, shape, where):
            return lax.dynamic_slice(array, where, shape, allow_negative_indices=False)

        zero = jnp.zeros_like(start)
        return jnp.concatenate(
            [
                part(cotangent, (HALO, width), (start, zero)),
                part(neighbours, (offsets, HALO), (zero, start)).astype(F32),
            ],
            0,
        )

    ext_shape = (rows + 2 * HALO, width)
    stats_shape = (count, 2, width)
    edge = (HALO, width)
    wide_edge = (2 * HALO + offsets, width)
    vector = (1, width)
    turned_rows = -(-offsets // 8) * 8
    taken = (offsets, 2 * width, rows)
    halves = (ext_shape[0], 2 * width)
    conv_scratch = [
        pltpu.VMEM(ext_shape, F32),
        pltpu.VMEM((offsets, width, width), F32),
        pltpu.VMEM(taken, BF16),
        pltpu.VMEM(ext_shape[::-1], F32),
        pltpu.VMEM(halves[::-1], BF16),
        pltpu.SemaphoreType.DMA((4,)),
    ]
    grad_scratch = [pltpu.VMEM(taken, BF16), pltpu.SemaphoreType.DMA((len(CHUNKS) - 1,))]
    x_edges = swap(
        *run(
            pack_kernel,
            cumulative,
            (("far", features),),
            (edge, edge),
            [pltpu.VMEM(edge, F32), pltpu.VMEM((HALO + 8, width), F32), pltpu.SemaphoreType.DMA((2,))],
        )
    )
    mores = (more(jnp.where(even, tail, 0)), more(jnp.where(even, 0, tail)))
    ring = Ring(count, offsets * width // 8)
    grad = (ring.padded, 8, width)
    work = 2 * offsets * rows * width * width * 4

    def move(piece, pairs):
        return lax.ppermute(piece, "vox", pairs)

    def near(shape, kind=F32):
        return ("near", shape, kind)

    y1, swap1, swap2, stats, stash1 = run(
        first_kernel,
        cumulative,
        (*x_edges, *mores, ("far", features), ("far", neighbours), ("far", kernel_one)),
        (near((rows, width)), wide_edge, wide_edge, stats_shape, ("far", taken, BF16)),
        [
            pltpu.VMEM(neighbours.shape, jnp.int32),
            pltpu.SemaphoreType.DMA((2,)),
            *conv_scratch,
        ],
        flops=3 * work,
    )
    y1_edges = swap(swap1, swap2)
    stats1 = spread(stats)
    y2, swap1, swap2, stats, stash2, target, later_target = run(
        second_kernel,
        cumulative,
        (y1, *y1_edges, stats1, gain_one, bias_one, neighbours, ("far", kernel_two)),
        (
            near((rows, width)), edge, edge, stats_shape, ("far", taken, BF16),
            near((turned_rows, ext_shape[0]), jnp.int32),
            ("far", (turned_rows, ext_shape[0]), jnp.int32),
        ),
        [
            pltpu.VMEM((ext_shape[0], turned_rows), jnp.int32),
            pltpu.SemaphoreType.DMA,
            *conv_scratch,
        ],
        flops=3 * work,
    )
    y2_edges = swap(swap1, swap2)
    stats2 = spread(stats)
    output, dz2, unit2, stats = run(
        middle_kernel,
        cumulative,
        (
            y2, *y2_edges, stats2, gain_two, bias_two, features, *x_edges, *y1_edges, cotangent,
        ),
        ((rows, width), near(ext_shape), near(ext_shape), stats_shape),
        [],
    )
    back2 = spread(stats)
    dy2, dpre, dz1, swap1, swap2, stats, dgain_two, dbias_two = run(
        back_two_kernel,
        cumulative,
        (
            dz2, unit2, stats2, back2, gain_two, target, y1, stats1, gain_one, bias_one,
            kernel_two,
        ),
        (
            ("far", (rows, width), F32), ("far", (rows, width), F32), near((rows, width)), edge,
            edge, stats_shape, vector, vector,
        ),
        [
            pltpu.VMEM(halves, BF16),
            pltpu.VMEM((2, rows, width), F32),
            pltpu.SemaphoreType.DMA((2,)),
        ],
        flops=3 * work,
    )
    dz_edges = swap(swap1, swap2)
    back1 = spread(stats)
    (two,) = run(
        functools.partial(grad_two_kernel, ring),
        None,
        (("far", dy2), ("far", stash2)),
        (near(grad),),
        [pltpu.VMEM((rows, width), F32), pltpu.SemaphoreType.DMA, *grad_scratch],
        flops=work,
    )
    keep, give, halves_one, dgain_one, dbias_one = run(
        functools.partial(grad_one_kernel, ring),
        cumulative,
        (
            dz1, *dz_edges, y1, *y1_edges, stats1, back1, gain_one, two, ("far", stash1),
        ),
        (grad, grad, near(halves, BF16), vector, vector),
        [pltpu.VMEM(ext_shape, F32), pltpu.VMEM(grad, F32), *grad_scratch],
        flops=work,
    )
    theirs = move(give, [(i, i ^ 1) for i in range(count)])
    dx = None
    blocks = list(range(rows // BLOCK))

    def beside(sent):
        nonlocal dx
        block = blocks.pop(0)
        arrays = (halves_one, later_target, dpre, kernel_one, ("any", sent))
        dx, zero = run(
            functools.partial(back_one_kernel, block),
            None,
            arrays if dx is None else (*arrays, ("far", dx)),
            (("far", (rows, width), F32), (8, width)),
            [pltpu.VMEM((BLOCK, width), F32), pltpu.SemaphoreType.DMA],
            flops=3 * work // (rows // BLOCK),
            aliases=None if dx is None else {len(arrays): 0},
        )
        return zero

    def part(array, w):
        return array[ring.starts[w] : ring.starts[w + 1]]

    sums = sum_chips(
        ring,
        [(part(keep, w), part(theirs, w)) for w in range(len(ring.orders))],
        lambda piece, bit: move(piece, [(i, i ^ (1 << bit)) for i in range(count)]),
        lambda piece: move(piece, [(i, i ^ 1) for i in range(count)]),
        beside,
        beside(give),
    )
    grads = run(
        functools.partial(finish_kernel, ring),
        None,
        [("any", piece) for piece in sums],
        (("far", grad, F32), ("far", grad, F32)),
        [pltpu.SemaphoreType.DMA((2,))],
    )
    dkernel_one, dkernel_two = (
        array[: ring.tiles].reshape(offsets, width, width) for array in grads
    )
    return (
        output,
        dx,
        dkernel_one,
        dkernel_two,
        dgain_one[0],
        dbias_one[0],
        dgain_two[0],
        dbias_two[0],
    )


def solution(mesh):
    return jax.shard_map(
        per_device,
        mesh=mesh,
        in_specs=(
            P("vox", None),
            P(),
            P(),
            P(),
            P(),
            P(),
            P(),
            P("vox", None),
            P(),
            P(None, "vox"),
        ),
        out_specs=(P("vox", None), P("vox", None), P(), P(), P(), P(), P(), P()),
        check_vma=False,
    )
```
